128 devices in a mesh: gx: 16 (over x, z), gy: 4 (over y_lo, core), gz: 2 (over y_hi).
Axes of the slice: x: 4, y: 4 (y_hi: 2, y_lo: 2; y = y_hi * 2 + y_lo), z: 4, core: 2. Of those that a mesh axis runs over, the one named last changes fastest.
Arguments:
- courant: float32 [512, 256, 512], P('gx', 'gy', 'gz'), may hold values from 0.06 to 0.19
- current: float32 [512, 256, 512], P('gx', 'gy', 'gz'), may hold values from -3 to 9
- previous: float32 [512, 256, 512], P('gx', 'gy', 'gz'), may hold values from -3 to 9
- image_in: float32 [512, 256, 512], P('gx', 'gy', 'gz'), may hold values from -6 to 6
- forward_tt: float32 [4, 512, 256, 512], P(None, 'gx', 'gy', 'gz'), may hold values from -4 to 4
- traces: float32 [32768, 4], P(('gx', 'gy', 'gz')), may hold values from -8 to 8
- trace_owner: int32 [32768, 1], P(('gx', 'gy', 'gz')), may hold values from 0 to 127; in each aligned block of 256 rows (0 to 255, 256 to 511, ...) at most 8 rows name the same one
- receiver_cell: int32 [32768], P(('gx', 'gy', 'gz')), may hold values from 0 to 524287
Outputs:
- image: float32 [512, 256, 512], P('gx', 'gy', 'gz')
- final_now: float32 [512, 256, 512], P('gx', 'gy', 'gz')
- final_before: float32 [512, 256, 512], P('gx', 'gy', 'gz')
The draws below stay inside these ranges and needn't reach their ends.
Inputs may be any that keep to these rules, and one draw needn't show every extreme that they name: `trace_owner`: tiles are numbered in gx, gy, gz order. Among the 256 rows of one device (aligned blocks), no tile is named by more than 8 rows, a bound that some block reaches. `receiver_cell`: cell x * 64 * 256 + y * 256 + z of the owner's tile.
All inputs are finite; a program needn't handle non-finite values.
Results may differ from the reference program's by a relative error of at most 0.00002.
Values sent between devices are 32-bit elements; how exact they have to be, the bound alone decides.
A program may use at most 384 MiB of HBM per device.

```python
import math
import jax
import jax.numpy as jnp
import numpy as np
from jax import lax

CX = 32
CY = 64
CZ = 256
STEPS = 4
REC_DEV = 256
CAP = 8
NX = 512
NY = 256
NZ = 512
RECS = 32768
N_GY = 4
N_GZ = 2
DEVICES = 128


def smooth_background(key, level_lo, level_hi):
    keys = jax.random.split(key, 2)
    level = jax.random.uniform(keys[0], (), jnp.float32, level_lo, level_hi)
    phase = jax.random.uniform(keys[1], (3,), jnp.float32, 0.0, 2.0 * math.pi)
    along_x = jnp.arange(NX, dtype=jnp.float32)[:, None, None]
    along_y = jnp.arange(NY, dtype=jnp.float32)[None, :, None]
    along_z = jnp.arange(NZ, dtype=jnp.float32)[None, None, :]
    wave = jnp.sin(2.0 * math.pi * along_x / NX + phase[0]) * jnp.cos(2.0 * math.pi * along_y / NY + phase[1]) * jnp.sin(2.0 * math.pi * along_z / NZ + phase[2])
    return level * (1.0 + 0.3 * wave)


def rough_part(key, limit):
    return jnp.clip(jax.random.normal(key, (NX, NY, NZ), jnp.float32), -limit, limit)


def draw_current(key, part):
    background = smooth_background(key, 1.5, 2.5)
    key = jax.random.fold_in(key, 11)
    return background + rough_part(key, 4.0)


def draw_previous(key, part):
    background = smooth_background(key, 1.5, 2.5)
    key = jax.random.fold_in(key, 23)
    return background + rough_part(key, 4.0)


def touch_ends(entries, own_key, least, high):
    index_at = [jax.random.randint(jax.random.fold_in(own_key, axis), (), 0, length) for axis, length in enumerate(entries.shape)]
    main_axis = entries.shape.index(max(entries.shape))
    next_to = index_at[:main_axis] + [(index_at[main_axis] + 1) % entries.shape[main_axis]] + index_at[main_axis + 1:]
    return entries.at[tuple(index_at)].set(least).at[tuple(next_to)].set(high)


def block_scale(stream_key, dims, cuts, low, largest):
    def one(axis_at, parts):
        steps = jax.random.uniform(jax.random.fold_in(jax.random.fold_in(stream_key, 6), axis_at), (parts,), jnp.float32, low / len(cuts), largest / len(cuts))
        return jnp.repeat(jnp.exp(steps), dims[axis_at] // parts).reshape((-1,) + (1,) * (len(dims) - axis_at - 1))

    level = one(*cuts[0])
    for cut in cuts[1:]:
        level = level * one(*cut)
    return level


def assign_block(rng, own, number, rows, amount, top, most, skew):
    sequence = jax.random.permutation(rng, amount)
    heavy_load, usual = load_shares(amount, rows * top, most, skew, True), load_shares(amount, rows * top, most, skew, False)
    places = jnp.arange(amount)

    def named(tallies, turn):
        used = int((tallies > 0).sum())
        fixed = max(1, used // 4)
        passed = fixed + (places - fixed + turn * (used - fixed)) % max(1, amount - fixed)
        return jnp.zeros((amount,), jnp.int32).at[sequence[jnp.where(places < fixed, places, passed)]].set(jnp.asarray(tallies, jnp.int32))

    tallies = jnp.where(number % 4 == 0, named(heavy_load, number // 4), named(usual, number - number // 4 - 1))
    mixed = jax.random.permutation(jax.random.fold_in(own, 3), amount)
    source_of, receiver = mixed[0:amount // 2 * 2:2], mixed[1:amount // 2 * 2:2]
    margin = jnp.minimum(tallies[source_of] - 1, most - tallies[receiver]) // 2
    margin = jnp.where((source_of == sequence[0]) | (receiver == sequence[0]) | (tallies[receiver] == 0), 0, jnp.maximum(margin, 0))
    passed = jax.random.randint(jax.random.fold_in(own, 4), (amount // 2,), 0, 1 << 20) % (margin + 1)
    tallies = tallies.at[source_of].add(-passed).at[receiver].add(passed)
    labels = jnp.searchsorted(jnp.cumsum(tallies), jnp.arange(rows * top), side="right").astype(jnp.int32)
    grid = labels.reshape(top, rows).T
    grid = grid[jax.random.permutation(jax.random.fold_in(own, 1), rows)]
    turn = jax.random.randint(jax.random.fold_in(own, 2), (rows, 1), 0, top)
    return jnp.take_along_axis(grid, (jnp.arange(top)[None, :] + turn) % top, axis=1)


def load_shares(amount, total, reach, slope, full):
    loads = [(1 << 20) // math.isqrt(standing ** slope) + 1 for standing in range(1, amount + 1)]
    largest = reach if full else min(reach, max(-(-total // amount), total * loads[0] // sum(loads)))
    least = 1 if total - largest >= amount - 1 else 0
    holding, rest = [largest] + [least] * (amount - 1), total - largest - least * (amount - 1)
    while rest > 0:
        free = [i for i in range(1, amount) if holding[i] < largest] or [i for i in range(1, amount) if holding[i] < reach]
        pool, remaining = sum([loads[i] for i in free]), rest
        for i in free:
            extra = min(reach - holding[i], max(1, remaining * loads[i] // pool), rest)
            holding[i] = holding[i] + extra
            rest = rest - extra
    return np.array(holding)


def bell_draw(own_key, shape, scale, most, cuts=(), kind=jnp.bfloat16):
    array = scale * jax.random.normal(own_key, shape, jnp.float32)
    if cuts:
        array = array * block_scale(own_key, shape, cuts, -0.22, 0.18)
    return jnp.clip(array, -most, most).astype(kind)


def setup_inputs(seed: int = 0) -> dict:
    key_of = jax.random.split(jax.random.key(seed), 9)
    courant = jnp.clip(jnp.exp(math.log(0.19) - 1.15267952 * jax.random.uniform(key_of[0], (NX, NY, NZ), jnp.float32) ** block_scale(key_of[0], (NX, NY, NZ), ((0, 16), (1, 4), (2, 2)), -0.2, 0.2)), 0.06, 0.19)
    current = draw_current(jax.random.fold_in(key_of[8], 71), 0)
    previous = draw_previous(jax.random.fold_in(key_of[8], 71), 0)
    image_in = bell_draw(key_of[3], (NX, NY, NZ), 1.0, 6.0, ((0, 16), (1, 4), (2, 2)), jnp.float32)
    forward_tt = bell_draw(key_of[4], (STEPS, NX, NY, NZ), 0.5, 4.0, ((1, 16), (2, 4), (3, 2)), jnp.float32)
    traces = bell_draw(key_of[5], (RECS, STEPS), 2.0, 8.0, ((0, 128),), jnp.float32)
    trace_owner_keys = jax.random.split(jax.random.fold_in(key_of[6], 1), RECS // REC_DEV)
    trace_owner_turns = jax.random.permutation(jax.random.fold_in(key_of[6], 3), RECS // REC_DEV)
    trace_owner = jax.vmap(lambda own, number: assign_block(jax.random.fold_in(key_of[6], 2), own, number, REC_DEV, DEVICES, 1, CAP, 2))(trace_owner_keys, trace_owner_turns).reshape((RECS, 1))
    receiver_cell = touch_ends(jax.random.randint(key_of[7], (RECS,), 0, CX * CY * CZ), jax.random.fold_in(key_of[7], 1), 0, (CX * CY * CZ) - 1).astype(jnp.int32)
    return dict(courant=courant, current=current, previous=previous, image_in=image_in, forward_tt=forward_tt, traces=traces, trace_owner=trace_owner, receiver_cell=receiver_cell)


taps = (-205.0 / 72.0, 8.0 / 5.0, -1.0 / 5.0, 8.0 / 315.0, -1.0 / 560.0)


def laplace(padded):
    radius = len(taps) - 1
    inner = [extent - 2 * radius for extent in padded.shape]

    def window(axis, offset):
        start = [radius, radius, radius]
        start[axis] = radius + offset
        limit = [begin + extent for begin, extent in zip(start, inner)]
        return lax.slice(padded, start, limit)

    total = (3.0 * taps[0]) * window(0, 0)
    for axis in range(3):
        for offset in range(1, radius + 1):
            total = total + taps[offset] * (window(axis, offset) + window(axis, -offset))
    return total


def reference(courant, current, previous, image_in, forward_tt, traces, trace_owner, receiver_cell):
    radius = len(taps) - 1
    owner = trace_owner[:, 0].astype(jnp.int32)
    tile_x = owner // (N_GY * N_GZ)
    tile_y = (owner // N_GZ) % N_GY
    tile_z = owner % N_GZ
    cell = receiver_cell.astype(jnp.int32)
    local_x = cell // (CY * CZ)
    local_y = (cell // CZ) % CY
    local_z = cell % CZ
    glob = ((tile_x * CX + local_x) * NY + tile_y * CY + local_y) * NZ + tile_z * CZ + local_z
    glob = glob.astype(jnp.int32)
    image = image_in
    for step in range(STEPS):
        source = jnp.zeros((NX * NY * NZ,), jnp.float32).at[glob].add(traces[:, step]).reshape(NX, NY, NZ)
        padded = jnp.pad(current, radius)
        updated = 2.0 * current - previous + courant * (laplace(padded) + source)
        image = image + forward_tt[step] * updated
        previous, current = current, updated
    return image, current, previous
```

```python
import functools

import jax
import jax.numpy as jnp
from jax import lax
from jax.experimental import pallas as pl
from jax.experimental.pallas import tpu as pltpu
from jax.sharding import PartitionSpec as P

STEPS = 4
CAP = 8
CX, CY, CZ = 32, 64, 256
N_GX, N_GY, N_GZ = 16, 4, 2
RECS = 256
CHUNKS = 4
ROWS = CY // CHUNKS
SCALE = 5040.0
TAPS = (0.0, 8064.0, -1008.0, 128.0, -9.0)
CENTRE = -43050.0
F32, BF16, I32 = jnp.float32, jnp.bfloat16, jnp.int32
MESH = pl.DeviceIdType.MESH


def split(v):
    hi = v.astype(BF16)
    return hi, (v - hi.astype(F32)).astype(BF16)


def tap_of(distance):
    out = jnp.zeros(distance.shape, F32)
    for offset in range(1, 5):
        out = jnp.where(distance == offset, TAPS[offset], out)
    return out


def dot(a, b):
    return lax.dot_general(a, b, (((1,), (0,)), ((), ())), preferred_element_type=F32)


def iota(shape, dim):
    return lax.broadcasted_iota(I32, shape, dim)


def kernel(courant, current, previous, image_in, forward, meta,
           image_out, now_out, before_out,
           u, cou, fwd, img, acc, onehot, dval, xh, ys, yr, zs, zr,
           band_z, band_y, edge_y, edge_z, r2t, packed, r1, t1, r2,
           in_sem, out_sem, xs_sem, xr_sem, ys_sem, yr_sem, zs_sem, zr_sem, route_sem):
    gx, gy, gz = lax.axis_index("gx"), lax.axis_index("gy"), lax.axis_index("gz")
    group = gy * N_GZ + gz

    loads = [
        pltpu.make_async_copy(current, u.at[1], in_sem.at[0]),
        pltpu.make_async_copy(previous, u.at[0], in_sem.at[1]),
        pltpu.make_async_copy(courant, cou, in_sem.at[2]),
        pltpu.make_async_copy(image_in, img, in_sem.at[3]),
    ] + [pltpu.make_async_copy(forward.at[k], fwd.at[k], in_sem.at[4 + k]) for k in range(STEPS)]
    for load in loads:
        load.start()

    barrier = pltpu.get_barrier_semaphore()

    def in_group(offset):
        other = lax.rem(group + offset, N_GY * N_GZ)
        return other, (gx, other // N_GZ, lax.rem(other, N_GZ))

    def in_line(offset):
        other = lax.rem(gx + offset, N_GX)
        return other, (other, gy, gz)

    def greet_group(o, carry):
        pl.semaphore_signal(barrier, inc=1, device_id=in_group(o)[1], device_id_type=MESH)
        return carry

    def greet_line(o, carry):
        pl.semaphore_signal(barrier, inc=1, device_id=in_line(o)[1], device_id_type=MESH)
        return carry

    lax.fori_loop(1, 8, greet_group, 0)
    lax.fori_loop(1, 16, greet_line, 0)

    r_, c_ = iota((CZ, CZ), 0), iota((CZ, CZ), 1)
    band_z[...] = tap_of(jnp.abs(r_ - c_)).astype(BF16)
    r_, c_ = iota((CY, 2 * CY), 0), iota((CY, 2 * CY), 1)
    band_y[...] = tap_of(jnp.abs(r_ - lax.rem(c_, CY))).astype(BF16)
    r_, c_ = iota((128, 256), 0), iota((128, 256), 1)
    c_ = lax.rem(c_, 128)
    h_, j_ = lax.rem(c_, 4), lax.rem(r_, 4)
    same = (c_ // 4) == (r_ // 4)
    edge_y[0] = jnp.where(same & (h_ >= j_), tap_of(4 - (h_ - j_)), 0.0).astype(BF16)
    edge_y[1] = jnp.where(same & (h_ <= j_), tap_of(4 - (j_ - h_)), 0.0).astype(BF16)
    r_, c_ = iota((128, 128), 0), iota((128, 128), 1)
    h_, j_ = lax.rem(r_, 4), lax.rem(c_, 4)
    same = (c_ // 4) == (r_ // 4)
    lower = jnp.where(same & (h_ >= j_), tap_of(4 - (h_ - j_)), 0.0)
    upper = jnp.where(same & (h_ <= j_), tap_of(4 - (j_ - h_)), 0.0)
    edge_z[...] = jnp.where(gz == 0, lower, upper).astype(BF16)

    @pl.when(gx == 0)
    def _():
        for k in range(STEPS):
            xh[k, 0] = jnp.zeros(xh.shape[2:], F32)

    @pl.when(gx == N_GX - 1)
    def _():
        for k in range(STEPS):
            xh[k, 1] = jnp.zeros(xh.shape[2:], F32)

    @pl.when(gy == 0)
    def _():
        for k in range(STEPS):
            yr[k, 0] = jnp.zeros(yr.shape[2:], F32)

    @pl.when(gy == N_GY - 1)
    def _():
        for k in range(STEPS):
            yr[k, 1] = jnp.zeros(yr.shape[2:], F32)

    owner_row = meta[4:5, :].astype(I32)
    place = (owner_row % 8) * 16 + owner_row // 8
    cell = meta[5:6, :].astype(I32)
    row = cell // CZ
    field = [None] * 16
    for k in range(STEPS):
        hi, lo = split(meta[k:k + 1, :] * SCALE)
        field[k], field[4 + k] = hi.astype(F32), lo.astype(F32)
    field[8] = (row // 256).astype(F32)
    field[9] = (row % 256).astype(F32)
    field[10] = (cell % CZ).astype(F32)
    zero = jnp.zeros((1, RECS), F32)
    field = jnp.concatenate([zero if f is None else f for f in field], axis=0)
    fields = jnp.concatenate([field] * 8, axis=0)
    owner_col = jnp.transpose(jnp.broadcast_to(meta[4:5, :], (128, RECS)))[:, :1]
    earlier = (owner_col == meta[4:5, :]) & (iota((RECS, RECS), 0) < iota((RECS, RECS), 1))
    rank = jnp.sum(jnp.where(earlier, 1.0, 0.0), axis=0, keepdims=True)
    mine = iota((128, RECS), 0) == place
    lane_block = iota((128, RECS), 0) // 16
    sums = jnp.zeros((128, 128), F32)
    for j in range(CAP):
        pick = jnp.where(mine & (rank == float(j)), 1.0, 0.0).astype(BF16)
        part = jnp.where(lane_block == j, fields, 0.0).astype(BF16)
        sums = sums + lax.dot_general(pick, part, (((1,), (1,)), ((), ())), preferred_element_type=F32)
    packed[...] = sums.reshape(8, 16, 128)

    pl.semaphore_wait(barrier, 22)

    def x_copy(k, c, side):
        rows = pl.ds(c * ROWS, ROWS)
        planes = pl.ds(CX - 4, 4) if side == 0 else pl.ds(0, 4)
        src = current.at[planes, rows] if k == 0 else u.at[k + 1, planes, rows]
        return pltpu.make_async_remote_copy(
            src_ref=src, dst_ref=xh.at[k, side, :, rows],
            send_sem=xs_sem.at[k, c, side], recv_sem=xr_sem.at[k, c, side],
            device_id=(gx + 1 if side == 0 else gx - 1, gy, gz), device_id_type=MESH)

    to_right, to_left = gx < N_GX - 1, gx > 0

    def x_start(k, c):
        pl.when(to_right)(lambda: x_copy(k, c, 0).start())
        pl.when(to_left)(lambda: x_copy(k, c, 1).start())

    def x_wait(k, c):
        pl.when(to_left)(lambda: x_copy(k, c, 0).wait_recv())
        pl.when(to_right)(lambda: x_copy(k, c, 1).wait_recv())

    def y_copy(k, side):
        return pltpu.make_async_remote_copy(
            src_ref=ys.at[k, side], dst_ref=yr.at[k, side],
            send_sem=ys_sem.at[k, side], recv_sem=yr_sem.at[k, side],
            device_id=(gx, gy + 1 if side == 0 else gy - 1, gz), device_id_type=MESH)

    def z_copy(k):
        return pltpu.make_async_remote_copy(
            src_ref=zs.at[k], dst_ref=zr.at[k], send_sem=zs_sem.at[k], recv_sem=zr_sem.at[k],
            device_id=(gx, gy, 1 - gz), device_id_type=MESH)

    up, down = gy < N_GY - 1, gy > 0

    for c in range(CHUNKS):
        x_start(0, c)

    def send_group(o, carry):
        other, device = in_group(o)
        pltpu.make_async_remote_copy(
            src_ref=packed.at[other], dst_ref=r1.at[o], send_sem=route_sem.at[0], recv_sem=route_sem.at[1],
            device_id=device, device_id_type=MESH).start()
        return carry

    lax.fori_loop(1, 8, send_group, 0)
    r1[0] = packed[group]

    lanes128 = iota((CY, 128), 1)
    row8 = iota((8, CZ), 0)

    def pack_edges(k):
        v = u.at[k + 1]
        for side in range(2):
            def pick(p, carry):
                if side == 0:
                    a, b = v[2 * p, CY - 8:CY, :], v[2 * p + 1, CY - 8:CY, :]
                    tile = jnp.where(row8 < 4, pltpu.roll(a, 4, 0), b)
                else:
                    a, b = v[2 * p, 0:8, :], v[2 * p + 1, 0:8, :]
                    tile = jnp.where(row8 < 4, a, pltpu.roll(b, 4, 0))
                ys[k, side, pl.ds(p * 8, 8), :] = tile
                return carry
            lax.fori_loop(0, CX // 2, pick, 0, unroll=4)
            hi, lo = split(ys[k, side])
            ys[k, side] = dot(edge_y[side], jnp.concatenate([hi, lo], axis=0))
        pl.when(up)(lambda: y_copy(k, 0).start())
        pl.when(down)(lambda: y_copy(k, 1).start())
        half = pl.ds(pl.multiple_of((1 - gz) * 128, 128), 128)
        first = 4 + gz * 124

        def gather(x, carry):
            moved = pltpu.roll(v[x, :, half], lax.rem(4 * x + first, 128), 1)
            return jnp.where(lanes128 // 4 == x, moved, carry)

        edge = lax.fori_loop(0, CX, gather, jnp.zeros((CY, 128), F32), unroll=4)
        hi, lo = split(edge)
        zs[k] = dot(hi, edge_z[...]) + dot(lo, edge_z[...])
        z_copy(k).start()

    def phase_a(k, with_source):
        def body(g, carry):
            planes = pl.ds(4 * g, 4)
            v = u[k + 1, planes].reshape(4 * CY, CZ)
            hi, lo = split(v)
            total = dot(hi, band_z[...]) + dot(lo, band_z[...]) + CENTRE * v
            for p in range(4):
                part = slice(p * CY, (p + 1) * CY)
                both = jnp.concatenate([hi[part], lo[part]], axis=0)
                acc[4 * g + p] = total[part] + dot(band_y[...], both)
            return carry
        lax.fori_loop(0, CX // 4, body, 0)

    def sources(k):
        def body(g, carry):
            rows = pl.ds(pl.multiple_of(g * 256, 256), 256)
            part = dot(onehot[rows, :], dval[k, 0]) + dot(onehot[rows, :], dval[k, 1])
            planes = pl.ds(4 * g, 4)
            acc[planes] = acc[planes] + part.reshape(4, CY, CZ)
            return carry
        lax.fori_loop(0, CX // 4, body, 0)

    def add_edges(k):
        pl.when(down)(lambda: y_copy(k, 0).wait_recv())
        pl.when(up)(lambda: y_copy(k, 1).wait_recv())

        def add(p, carry):
            top = yr[k, 0, pl.ds(p * 8, 8), :]
            end = yr[k, 1, pl.ds(p * 8, 8), :]
            acc[2 * p, 0:8, :] += jnp.where(row8 < 4, top, 0.0)
            acc[2 * p + 1, 0:8, :] += jnp.where(row8 < 4, pltpu.roll(top, 4, 0), 0.0)
            acc[2 * p, CY - 8:CY, :] += jnp.where(row8 < 4, 0.0, pltpu.roll(end, 4, 0))
            acc[2 * p + 1, CY - 8:CY, :] += jnp.where(row8 < 4, 0.0, end)
            return carry
        lax.fori_loop(0, CX // 2, add, 0, unroll=4)

        z_copy(k).wait_recv()
        half = pl.ds(pl.multiple_of((1 - gz) * 128, 128), 128)
        got = zr[k]
        inside = jnp.where(gz == 0, 1, 0) * 31 == lanes128 // 4
        first = 128 + (1 - gz) * 124

        def spread(x, carry):
            moved = pltpu.roll(got, lax.rem(first - 4 * x, 128), 1)
            acc[x, :, half] += jnp.where(inside, moved, 0.0)
            return carry
        lax.fori_loop(0, CX, spread, 0, unroll=4)

    def update(k, planes, window, rows):
        for x in planes:
            v = window(x)
            total = acc[x, rows, :]
            for o in range(1, 5):
                total = total + TAPS[o] * (window(x - o) + window(x + o))
            new = (v + v) - u[k, x, rows, :] + cou[x, rows, :] * total
            u[k + 2, x, rows, :] = new
            img[x, rows, :] = img[x, rows, :] + fwd[k, x, rows, :] * new

    def inner(k):
        def body(t, carry):
            rows = pl.ds(pl.multiple_of(t * 8, 8), 8)
            planes = {x: u[k + 1, x, rows, :] for x in range(CX)}
            update(k, range(4, CX - 4), lambda x: planes[x], rows)
            return carry
        lax.fori_loop(0, CY // 8, body, 0)

    def outer(k, c):
        def body(t, carry):
            rows = pl.ds(pl.multiple_of(t * 8, 8), 8)
            for side in range(2):
                low = 0 if side == 0 else CX - 8
                planes = {x: u[k + 1, x, rows, :] for x in range(low, low + 8)}
                for i in range(4):
                    planes[i - 4 if side == 0 else CX + i] = xh[k, side, i, rows, :]
                here = range(0, 4) if side == 0 else range(CX - 4, CX)
                update(k, here, lambda x: planes[x], rows)
            return carry
        lax.fori_loop(c * ROWS // 8, (c + 1) * ROWS // 8, body, 0)

    def route():
        pltpu.make_async_copy(r1.at[pl.ds(1, 7)], r1.at[pl.ds(1, 7)], route_sem.at[1]).wait()
        for g in range(N_GX):
            t1[g] = r1[:, g, :]

        def send_line(o, carry):
            other, device = in_line(o)
            pltpu.make_async_remote_copy(
                src_ref=t1.at[other], dst_ref=r2.at[o], send_sem=route_sem.at[2], recv_sem=route_sem.at[3],
                device_id=device, device_id_type=MESH).start()
            return carry
        lax.fori_loop(1, 16, send_line, 0)
        r2[0] = t1[gx]

    def unpack():
        pltpu.make_async_copy(r2.at[pl.ds(1, 15)], r2.at[pl.ds(1, 15)], route_sem.at[3]).wait()
        got = r2[...].reshape(128, 128)
        r2t[...] = jnp.transpose(got)

        def mark(r, carry):
            wanted = r2t[pl.ds(16 * r + 8, 1), :] * 256.0 + r2t[pl.ds(16 * r + 9, 1), :]
            wanted = wanted.astype(I32)
            columns = pl.ds(pl.multiple_of(128 * r, 128), 128)

            def rows_of(g, carry):
                hit = iota((256, 128), 0) + g * 256 == wanted
                onehot[pl.ds(pl.multiple_of(g * 256, 256), 256), columns] = jnp.where(hit, 1.0, 0.0).astype(BF16)
                return carry
            lax.fori_loop(0, 8, rows_of, 0)

            mine = pltpu.roll(got, lax.rem(128 - 16 * r, 128), 1)
            hit = iota((128, CZ), 1) == mine[:, 10:11].astype(I32)
            for k in range(STEPS):
                for piece in range(2):
                    f = 4 * piece + k
                    dval[k, piece, columns, :] = jnp.where(hit, mine[:, f:f + 1], 0.0).astype(BF16)
            return carry
        lax.fori_loop(0, CAP, mark, 0)

    loads[0].wait()
    pack_edges(0)
    route()
    phase_a(0, False)
    loads[2].wait()

    def rescale(x, carry):
        cou[x] = cou[x] * (1.0 / SCALE)
        return carry
    lax.fori_loop(0, CX, rescale, 0)
    unpack()
    loads[1].wait()
    loads[3].wait()

    for k in range(STEPS):
        if k:
            pack_edges(k)
            phase_a(k, True)
        sources(k)
        add_edges(k)
        loads[4 + k].wait()
        inner(k)
        for c in range(CHUNKS):
            x_wait(k, c)
            outer(k, c)
            if k < STEPS - 1:
                x_start(k + 1, c)
        if k == STEPS - 2:
            keep = pltpu.make_async_copy(u.at[STEPS], before_out, out_sem.at[0])
            keep.start()

    stores = [
        pltpu.make_async_copy(u.at[STEPS + 1], now_out, out_sem.at[1]),
        pltpu.make_async_copy(img, image_out, out_sem.at[2]),
    ]
    for store in stores:
        store.start()

    pltpu.make_async_copy(r1.at[pl.ds(1, 7)], r1.at[pl.ds(1, 7)], route_sem.at[0]).wait()
    pltpu.make_async_copy(r2.at[pl.ds(1, 15)], r2.at[pl.ds(1, 15)], route_sem.at[2]).wait()
    for k in range(STEPS):
        for c in range(CHUNKS):
            pl.when(to_right)(lambda: x_copy(k, c, 0).wait_send())
            pl.when(to_left)(lambda: x_copy(k, c, 1).wait_send())
        pl.when(up)(lambda: y_copy(k, 0).wait_send())
        pl.when(down)(lambda: y_copy(k, 1).wait_send())
        z_copy(k).wait_send()
    keep.wait()
    for store in stores:
        store.wait()


def local(courant, current, previous, image_in, forward_tt, traces, trace_owner, receiver_cell):
    meta = jnp.concatenate([
        traces.T,
        trace_owner.T.astype(F32),
        receiver_cell[None, :].astype(F32),
        jnp.zeros((2, RECS), F32),
    ], axis=0)
    tile = jax.ShapeDtypeStruct((CX, CY, CZ), F32)
    dma = pltpu.SemaphoreType.DMA
    anywhere = pl.BlockSpec(memory_space=pl.ANY)
    return pl.pallas_call(
        kernel,
        out_shape=(tile, tile, tile),
        in_specs=[anywhere] * 5 + [pl.BlockSpec(memory_space=pltpu.VMEM)],
        out_specs=(anywhere,) * 3,
        scratch_shapes=[
            pltpu.VMEM((STEPS + 2, CX, CY, CZ), F32),
            pltpu.VMEM((CX, CY, CZ), F32),
            pltpu.VMEM((STEPS, CX, CY, CZ), F32),
            pltpu.VMEM((CX, CY, CZ), F32),
            pltpu.VMEM((CX, CY, CZ), F32),
            pltpu.VMEM((CX * CY, 128 * CAP), BF16),
            pltpu.VMEM((STEPS, 2, 128 * CAP, CZ), BF16),
            pltpu.VMEM((STEPS, 2, 4, CY, CZ), F32),
            pltpu.VMEM((STEPS, 2, 128, CZ), F32),
            pltpu.VMEM((STEPS, 2, 128, CZ), F32),
            pltpu.VMEM((STEPS, CY, 128), F32),
            pltpu.VMEM((STEPS, CY, 128), F32),
            pltpu.VMEM((CZ, CZ), BF16),
            pltpu.VMEM((CY, 2 * CY), BF16),
            pltpu.VMEM((2, 128, 256), BF16),
            pltpu.VMEM((128, 128), BF16),
            pltpu.VMEM((128, 128), F32),
            pltpu.VMEM((8, 16, 128), F32),
            pltpu.VMEM((8, 16, 128), F32),
            pltpu.VMEM((16, 8, 128), F32),
            pltpu.VMEM((16, 8, 128), F32),
            dma((4 + STEPS,)),
            dma((3,)),
            dma((STEPS, CHUNKS, 2)),
            dma((STEPS, CHUNKS, 2)),
            dma((STEPS, 2)),
            dma((STEPS, 2)),
            dma((STEPS,)),
            dma((STEPS,)),
            dma((4,)),
        ],
        compiler_params=pltpu.CompilerParams(
            collective_id=0, has_side_effects=True, vmem_limit_bytes=60 * 1024 * 1024),
    )(courant, current, previous, image_in, forward_tt, meta)


def solution(mesh):
    cells = P("gx", "gy", "gz")
    every = ("gx", "gy", "gz")
    return jax.shard_map(
        local,
        mesh=mesh,
        in_specs=(cells, cells, cells, cells, P(None, "gx", "gy", "gz"), P(every, None), P(every, None), P(every)),
        out_specs=(cells, cells, cells),
        check_vma=False,
    )
```

```python
from types import SimpleNamespace

import jax
import jax.numpy as jnp
from jax import lax
from jax.experimental import pallas as pl
from jax.experimental.pallas import tpu as pltpu
from jax.sharding import PartitionSpec as P

STEPS = 4
CAP = 8
CX, CY, CZ = 32, 64, 256
N_GX, N_GY, N_GZ = 16, 4, 2
RECS = 256
ROWS = 16
CHUNKS = (1, 2, 0, 3)
SCALE = 5040.0
TAPS = (0.0, 8064.0, -1008.0, 128.0, -9.0)
CENTRE = -43050.0
F32, BF16, I32 = jnp.float32, jnp.bfloat16, jnp.int32
MESH = pl.DeviceIdType.MESH


def split(v):
    hi = v.astype(BF16)
    return hi, (v - hi.astype(F32)).astype(BF16)


def tap_of(distance):
    out = jnp.zeros(distance.shape, F32)
    for offset in range(1, 5):
        out = jnp.where(distance == offset, TAPS[offset], out)
    return out


def dot(a, b):
    return lax.dot_general(a, b, (((1,), (0,)), ((), ())), preferred_element_type=F32)


def iota(shape, dim):
    return lax.broadcasted_iota(I32, shape, dim)


PARTS = ((0, 7), (1, 2, 3, 4, 5, 6))
PAIRS = ((0, 1, 14, 15), tuple(range(2, 14)))
Y_ROWS = ((0, 32), (32, 96))
TILE = (CX, CY, CZ)
MIB = 1024 * 1024


def pick_from(values, i):
    out = i + values[0]
    for n in range(1, len(values)):
        if values[n] != values[n - 1] + 1:
            out = jnp.where(i >= n, i - n + values[n], out)
    return out


def edges(n, shift, downward):
    r_, c_ = iota((n, n), 0), iota((n, n), 1)
    same = (c_ // 4) == lax.rem(r_ // 4 + shift, n // 4)
    gap = lax.rem(r_, 4) - lax.rem(c_, 4)
    gap = jnp.where(downward, gap, -gap)
    return jnp.where(same & (gap >= 0), tap_of(4 - gap), 0.0)


def place():
    at = SimpleNamespace(gx=lax.axis_index("gx"), gy=lax.axis_index("gy"), gz=lax.axis_index("gz"))
    at.right, at.left = at.gx < N_GX - 1, at.gx > 0
    at.up, at.down = at.gy < N_GY - 1, at.gy > 0
    return at


def faces(at, ys, yr, zs, zr, ys_sem, yr_sem, zs_sem, zr_sem, weights):
    band_z, band_y, edge_y, edge_y_few, edge_z = weights
    block_of_lane = iota((CY, 128), 1) // 4
    own_block = lax.rem(block_of_lane + 32 - at.gz, 32)
    inside = block_of_lane == 31 * (1 - at.gz)
    row8 = iota((8, CZ), 0)
    half = pl.ds(pl.multiple_of((1 - at.gz) * 128, 128), 128)

    def y_copy(n, part, side):
        rows = pl.ds(*Y_ROWS[part])
        return pltpu.make_async_remote_copy(
            src_ref=ys.at[n, side, rows], dst_ref=yr.at[n, side, rows],
            send_sem=ys_sem.at[n, part, side], recv_sem=yr_sem.at[n, part, side],
            device_id=(at.gx, at.gy + 1 if side == 0 else at.gy - 1, at.gz), device_id_type=MESH)

    def z_copy(n, part):
        return pltpu.make_async_remote_copy(
            src_ref=zs.at[n, part], dst_ref=zr.at[n, part],
            send_sem=zs_sem.at[n, part], recv_sem=zr_sem.at[n, part],
            device_id=(at.gx, at.gy, 1 - at.gz), device_id_type=MESH)

    def clear(slots):
        @pl.when(at.gy == 0)
        def _():
            for n in range(slots):
                yr[n, 0] = jnp.zeros(yr.shape[2:], F32)

        @pl.when(at.gy == N_GY - 1)
        def _():
            for n in range(slots):
                yr[n, 1] = jnp.zeros(yr.shape[2:], F32)

    def send(n, part, v):
        first, count = Y_ROWS[part]
        packed_rows = []
        for p in PAIRS[part]:
            a, b = v[2 * p, CY - 8:CY, :], v[2 * p + 1, CY - 8:CY, :]
            packed_rows.append(jnp.where(row8 < 4, pltpu.roll(a, 4, 0), b))
        for p in PAIRS[part]:
            a, b = v[2 * p, 0:8, :], v[2 * p + 1, 0:8, :]
            packed_rows.append(jnp.where(row8 < 4, a, pltpu.roll(b, 4, 0)))
        hi, lo = split(jnp.concatenate(packed_rows, axis=0))
        matrix = edge_y[...] if part else edge_y_few[...]
        sums = dot(matrix, hi) + dot(matrix, lo)
        for side in range(2):
            ys[n, side, first:first + count, :] = sums[side * count:(side + 1) * count]
        pl.when(at.up)(lambda: y_copy(n, part, 0).start())
        pl.when(at.down)(lambda: y_copy(n, part, 1).start())

        edge = jnp.zeros((CY, 128), F32)
        for g in PARTS[part]:
            for x in range(4 * g, 4 * g + 4):
                moved = pltpu.roll(v[x, :, half], (4 * x + 4) % 128, 1)
                edge = jnp.where(own_block == x, moved, edge)
        hi, lo = split(edge)
        zs[n, part] = dot(hi, edge_z[...]) + dot(lo, edge_z[...])
        z_copy(n, part).start()

    def add(n, part, total):
        pl.when(at.down)(lambda: y_copy(n, part, 0).wait_recv())
        pl.when(at.up)(lambda: y_copy(n, part, 1).wait_recv())
        first, count = Y_ROWS[part]
        for i, p in enumerate(PAIRS[part]):
            top = yr[n, 0, first + i * 8:first + i * 8 + 8, :]
            end = yr[n, 1, first + i * 8:first + i * 8 + 8, :]
            total[2 * p, 0:8, :] += jnp.where(row8 < 4, top, 0.0)
            total[2 * p + 1, 0:8, :] += jnp.where(row8 < 4, pltpu.roll(top, 4, 0), 0.0)
            total[2 * p, CY - 8:CY, :] += jnp.where(row8 < 4, 0.0, pltpu.roll(end, 4, 0))
            total[2 * p + 1, CY - 8:CY, :] += jnp.where(row8 < 4, 0.0, end)
        z_copy(n, part).wait_recv()
        got = zr[n, part]
        for g in PARTS[part]:
            for x in range(4 * g, 4 * g + 4):
                moved = pltpu.roll(got, (128 - 4 * x) % 128, 1)
                total[x, :, half] += jnp.where(inside, moved, 0.0)

    def wait_sent(slots):
        for n in range(slots):
            for part in range(2):
                pl.when(at.up)(lambda: y_copy(n, part, 0).wait_send())
                pl.when(at.down)(lambda: y_copy(n, part, 1).wait_send())
                z_copy(n, part).wait_send()

    def bands(part, v_at, total):
        def body(i, carry):
            g = pick_from(PARTS[part], i)
            v = v_at[pl.ds(4 * g, 4)].reshape(4 * CY, CZ)
            hi, lo = split(v)
            here = dot(hi, band_z[...]) + dot(lo, band_z[...]) + CENTRE * v
            for p in range(4):
                rows = slice(p * CY, (p + 1) * CY)
                both = jnp.concatenate([hi[rows], lo[rows]], axis=0)
                total[4 * g + p] = here[rows] + dot(band_y[...], both)
            return carry
        lax.fori_loop(0, len(PARTS[part]), body, 0)

    return SimpleNamespace(clear=clear, send=send, add=add, wait_sent=wait_sent, bands=bands)


def x_copy(at, src, dst, sems, k, c, side):
    rows = pl.ds(c * ROWS, ROWS)
    planes = pl.ds(CX - 4, 4) if side == 0 else pl.ds(0, 4)
    return pltpu.make_async_remote_copy(
        src_ref=src.at[planes, rows], dst_ref=dst.at[side, :, rows],
        send_sem=sems[0].at[k, c, side], recv_sem=sems[1].at[k, c, side],
        device_id=(at.gx + 1 if side == 0 else at.gx - 1, at.gy, at.gz), device_id_type=MESH)


def first_kernel(current, previous, courant, image_in, traces, owners, cells,
                 cur, prev, cou, img, total, halo, values, targets,
                 band_z, band_y, edge_y, edge_y_few, edge_z,
                 tr, ow, ce, packed, r1, t1, r2, ys, yr, zs, zr,
                 in_sem, xs_sem, xr_sem, ys_sem, yr_sem, zs_sem, zr_sem, route_sem):
    at = place()
    group = at.gy * N_GZ + at.gz
    loads = [
        pltpu.make_async_copy(traces, tr, in_sem.at[0]),
        pltpu.make_async_copy(owners, ow, in_sem.at[1]),
        pltpu.make_async_copy(cells, ce, in_sem.at[2]),
        pltpu.make_async_copy(current, cur, in_sem.at[3]),
        pltpu.make_async_copy(courant, cou, in_sem.at[4]),
        pltpu.make_async_copy(previous, prev, in_sem.at[5]),
        pltpu.make_async_copy(image_in, img, in_sem.at[6]),
    ]
    for load in loads:
        load.start()

    barrier = pltpu.get_barrier_semaphore()

    def in_group(offset):
        other = lax.rem(group + offset, N_GY * N_GZ)
        return other, (at.gx, other // N_GZ, lax.rem(other, N_GZ))

    def in_line(offset):
        other = lax.rem(at.gx + offset, N_GX)
        return other, (other, at.gy, at.gz)

    def greet_group(o, carry):
        pl.semaphore_signal(barrier, inc=1, device_id=in_group(o)[1], device_id_type=MESH)
        return carry

    def greet_line(o, carry):
        pl.semaphore_signal(barrier, inc=1, device_id=in_line(o)[1], device_id_type=MESH)
        return carry

    lax.fori_loop(1, 16, greet_line, 0)
    lax.fori_loop(1, 8, greet_group, 0)

    for load in loads[:3]:
        load.wait()
    owner = ow[...]
    cell = ce[...]
    row = cell // CZ
    field = [None] * 16
    for k in range(STEPS):
        hi, lo = split(tr[k:k + 1, :] * SCALE)
        field[k], field[4 + k] = hi.astype(F32), lo.astype(F32)
    field[8] = (row // 256).astype(F32)
    field[9] = (row % 256).astype(F32)
    field[10] = (cell % CZ).astype(F32)
    field[11] = jnp.ones((1, RECS), F32)
    zero = jnp.zeros((1, RECS), F32)
    field = jnp.concatenate([zero if f is None else f for f in field], axis=0)
    fields = jnp.concatenate([field] * 8, axis=0)
    owner_f = owner.astype(F32)
    owner_col = jnp.transpose(jnp.broadcast_to(owner_f, (128, RECS)))[:, :1]
    earlier = (owner_col == owner_f) & (iota((RECS, RECS), 0) < iota((RECS, RECS), 1))
    rank = jnp.sum(jnp.where(earlier, 1.0, 0.0), axis=0, keepdims=True)
    mine = iota((128, RECS), 0) == owner
    lane_block = iota((128, RECS), 0) // 16
    sums = jnp.zeros((128, 128), F32)
    for j in range(CAP):
        pick = jnp.where(mine & (rank == float(j)), 1.0, 0.0).astype(BF16)
        part = jnp.where(lane_block == j, fields, 0.0).astype(BF16)
        sums = sums + lax.dot_general(pick, part, (((1,), (1,)), ((), ())), preferred_element_type=F32)
    packed[...] = sums.reshape(16, 8, 128)

    pl.semaphore_wait(barrier, 22)

    def send_line(o, carry):
        other, device = in_line(o)
        pltpu.make_async_remote_copy(
            src_ref=packed.at[other], dst_ref=r1.at[o], send_sem=route_sem.at[0], recv_sem=route_sem.at[1],
            device_id=device, device_id_type=MESH).start()
        return carry

    lax.fori_loop(1, 16, send_line, 0)

    def x_face(c, side):
        return x_copy(at, current, halo, (xs_sem, xr_sem), 0, c, side)

    for c in CHUNKS:
        pl.when(at.right)(lambda: x_face(c, 0).start())
        pl.when(at.left)(lambda: x_face(c, 1).start())
    r1[0] = packed[at.gx]

    r_, c_ = iota((CZ, CZ), 0), iota((CZ, CZ), 1)
    band_z[...] = tap_of(jnp.abs(r_ - c_)).astype(BF16)
    r_, c_ = iota((CY, 2 * CY), 0), iota((CY, 2 * CY), 1)
    band_y[...] = tap_of(jnp.abs(r_ - lax.rem(c_, CY))).astype(BF16)
    edge_z[...] = edges(128, 30 * at.gz, at.gz == 0).astype(BF16)
    for matrix, n in ((edge_y_few, 64), (edge_y, 192)):
        upward = iota((n, n), 0) < n // 2
        matrix[...] = edges(n, 0, ~upward).astype(BF16)

    face = faces(at, ys, yr, zs, zr, ys_sem, yr_sem, zs_sem, zr_sem,
                 (band_z, band_y, edge_y, edge_y_few, edge_z))
    face.clear(1)
    pl.when(~at.left)(lambda: halo.__setitem__(0, jnp.zeros(halo.shape[1:], F32)))
    pl.when(~at.right)(lambda: halo.__setitem__(1, jnp.zeros(halo.shape[1:], F32)))

    loads[3].wait()
    face.send(0, 0, cur)
    face.send(0, 1, cur)

    pltpu.make_async_copy(r1.at[pl.ds(1, 15)], r1.at[pl.ds(1, 15)], route_sem.at[1]).wait()
    for j in range(8):
        t1[j] = r1[:, j, :]

    def send_group(o, carry):
        other, device = in_group(o)
        pltpu.make_async_remote_copy(
            src_ref=t1.at[other], dst_ref=r2.at[o], send_sem=route_sem.at[2], recv_sem=route_sem.at[3],
            device_id=device, device_id_type=MESH).start()
        return carry

    lax.fori_loop(1, 8, send_group, 0)
    r2[0] = t1[group]

    face.bands(0, cur, total)
    face.bands(1, cur, total)
    loads[4].wait()

    def rescale(x, carry):
        cou[x] = cou[x] * (1.0 / SCALE)
        return carry
    lax.fori_loop(0, CX, rescale, 0)
    face.add(0, 0, total)
    face.add(0, 1, total)

    pltpu.make_async_copy(r2.at[pl.ds(1, 7)], r2.at[pl.ds(1, 7)], route_sem.at[3]).wait()
    got = jnp.transpose(r2[...].reshape(128, 128))
    for r in range(CAP):
        values[4 * r:4 * r + 4, :] = got[16 * r:16 * r + 4] + got[16 * r + 4:16 * r + 8]
        cell_row = (got[16 * r + 8:16 * r + 9] * 256.0 + got[16 * r + 9:16 * r + 10]).astype(I32)
        depth = got[16 * r + 10:16 * r + 11].astype(I32)
        targets[r:r + 1, :] = (cell_row // CY) * (2 * CY) + (depth // 128) * CY + cell_row % CY
        targets[CAP + r:CAP + r + 1, :] = depth % 128
    held = got[11:12]
    for r in range(1, CAP):
        held = held + got[16 * r + 11:16 * r + 12]
    targets[2 * CAP:2 * CAP + 1, :] = held.astype(I32)
    targets[2 * CAP + 1:, :] = jnp.zeros((7, 128), I32)

    for load in loads[5:]:
        load.wait()
    for c in CHUNKS:
        pl.when(at.left)(lambda: x_face(c, 0).wait_recv())
        pl.when(at.right)(lambda: x_face(c, 1).wait_recv())
        pl.when(at.right)(lambda: x_face(c, 0).wait_send())
        pl.when(at.left)(lambda: x_face(c, 1).wait_send())
    pltpu.make_async_copy(r1.at[pl.ds(1, 15)], r1.at[pl.ds(1, 15)], route_sem.at[0]).wait()
    pltpu.make_async_copy(r2.at[pl.ds(1, 7)], r2.at[pl.ds(1, 7)], route_sem.at[2]).wait()
    face.wait_sent(1)


def source_kernel(values, targets, source, field, spread, where, sem):
    fetch = pltpu.make_async_copy(targets, where, sem)
    fetch.start()
    rows = field.reshape(CX * 2 * CY * STEPS, 128)

    def blank(i, carry):
        rows[pl.ds(pl.multiple_of(i * 512, 512), 512), :] = jnp.zeros((512, 128), F32)
        return carry
    lax.fori_loop(0, CX * 2 * CY * STEPS // 512, blank, 0)
    for p in range(128):
        spread[p] = jnp.broadcast_to(values[:, p:p + 1], (CAP * STEPS, 128))
    fetch.wait()
    lanes = iota((STEPS, 128), 1)

    def put(entries):
        row = [where[r, p] for p, r in entries]
        part = [jnp.where(lanes == where[CAP + r, p], spread[p, STEPS * r:STEPS * (r + 1), :], 0.0) for p, r in entries]
        old = [field[i] for i in row]
        for i in range(len(entries)):
            total = old[i] + part[i]
            for j in range(len(entries)):
                if j != i:
                    total = total + jnp.where(row[i] == row[j], part[j], 0.0)
            old[i] = total
        for i in range(len(entries)):
            field[row[i]] = old[i]

    def two(i, carry):
        a, b = 2 * i, 2 * i + 1
        put(((a, 0), (a, 1), (b, 0), (b, 1)))

        @pl.when((where[2 * CAP, a] > 2) | (where[2 * CAP, b] > 2))
        def _():
            put(((a, 2), (a, 3), (b, 2), (b, 3)))

            @pl.when((where[2 * CAP, a] > 4) | (where[2 * CAP, b] > 4))
            def _():
                put(((a, 4), (a, 5), (b, 4), (b, 5)))
                put(((a, 6), (a, 7), (b, 6), (b, 7)))
        return carry
    lax.fori_loop(0, 64, two, 0)

    def arrange(x, carry):
        for k in range(STEPS):
            for h in range(2):
                for t in range(CY // 8):
                    first = ((x * 2 + h) * CY + t * 8) * STEPS + k
                    source[k, x, 8 * t:8 * t + 8, 128 * h:128 * h + 128] = rows[pl.ds(first, 8, stride=STEPS), :]
        return carry
    lax.fori_loop(0, CX, arrange, 0)


def update(planes, rows, window, before, after, cou, fwd, image, image_after, totals):
    for x in planes:
        v = window(x)
        total = totals[0][x, rows, :]
        for more in totals[1:]:
            total = total + more[x, rows, :]
        for o in range(1, 5):
            total = total + TAPS[o] * (window(x - o) + window(x + o))
        new = (v + v) - before[x, rows, :] + cou[x, rows, :] * total
        after[x, rows, :] = new
        image_after[x, rows, :] = image[x, rows, :] + fwd[x, rows, :] * new


def inner(v, *rest):
    def body(t, carry):
        rows = pl.ds(pl.multiple_of(t * 8, 8), 8)
        planes = {x: v[x, rows, :] for x in range(CX)}
        update(range(4, CX - 4), rows, lambda x: planes[x], *rest)
        return carry
    lax.fori_loop(0, CY // 8, body, 0)


def outer(c, halo, v, *rest):
    def body(t, carry):
        rows = pl.ds(pl.multiple_of(t * 8, 8), 8)
        for side in range(2):
            low = 0 if side == 0 else CX - 8
            planes = {x: v[x, rows, :] for x in range(low, low + 8)}
            for i in range(4):
                planes[i - 4 if side == 0 else CX + i] = halo[side, i, rows, :]
            here = range(0, 4) if side == 0 else range(CX - 4, CX)
            update(here, rows, lambda x: planes[x], *rest)
        return carry
    lax.fori_loop(c * ROWS // 8, (c + 1) * ROWS // 8, body, 0)


def step_kernel(cur, prev, cou, img_in, forward, total0, halo0, source, band_z, band_y, edge_y, edge_y_few, edge_z,
                now2, now3, total, img, halo3, fwd3,
                fwd, now1, halos, ys, yr, zs, zr,
                in_sem, xs_sem, xr_sem, ys_sem, yr_sem, zs_sem, zr_sem):
    at = place()
    loads = [pltpu.make_async_copy(forward.at[k], fwd3 if k == STEPS - 1 else fwd.at[k], in_sem.at[k]) for k in range(STEPS)]
    for load in loads:
        load.start()
    barrier = pltpu.get_barrier_semaphore()

    def greet(x, y, z):
        pl.semaphore_signal(barrier, inc=1, device_id=(x, y, z), device_id_type=MESH)

    pl.when(at.right)(lambda: greet(at.gx + 1, at.gy, at.gz))
    pl.when(at.left)(lambda: greet(at.gx - 1, at.gy, at.gz))
    pl.when(at.up)(lambda: greet(at.gx, at.gy + 1, at.gz))
    pl.when(at.down)(lambda: greet(at.gx, at.gy - 1, at.gz))
    greet(at.gx, at.gy, 1 - at.gz)
    one = lambda yes: jnp.where(yes, 1, 0)
    neighbours = 1 + one(at.right) + one(at.left) + one(at.up) + one(at.down)

    v_at = [prev, cur, now1, now2, now3]
    halo = [halo0, halos.at[0], halos.at[1], halo3]
    face = faces(at, ys, yr, zs, zr, ys_sem, yr_sem, zs_sem, zr_sem,
                 (band_z, band_y, edge_y, edge_y_few, edge_z))

    def rest(k):
        totals = (total0, source.at[0]) if k == 0 else (total, source.at[k])
        return (v_at[k], v_at[k + 2], cou, fwd.at[k], img_in if k == 0 else img, img, totals)

    def x_face(k, c, side):
        return x_copy(at, v_at[k + 1], halo[k], (xs_sem, xr_sem), k - 1, c, side)

    def x_start(k, c):
        pl.when(at.right)(lambda: x_face(k, c, 0).start())
        pl.when(at.left)(lambda: x_face(k, c, 1).start())

    def x_wait(k, c):
        pl.when(at.left)(lambda: x_face(k, c, 0).wait_recv())
        pl.when(at.right)(lambda: x_face(k, c, 1).wait_recv())

    face.clear(STEPS - 1)
    for k in range(1, STEPS):
        pl.when(~at.left)(lambda: halo[k].__setitem__(0, jnp.zeros(halo3.shape[1:], F32)))
        pl.when(~at.right)(lambda: halo[k].__setitem__(1, jnp.zeros(halo3.shape[1:], F32)))

    loads[0].wait()
    for c in CHUNKS:
        outer(c, halo0, cur, *rest(0))
    pl.semaphore_wait(barrier, neighbours)
    for c in CHUNKS:
        x_start(1, c)
    face.send(0, 0, now1)
    inner(cur, *rest(0))
    for k in range(1, STEPS - 1):
        v = v_at[k + 1]
        face.send(k - 1, 1, v)
        face.bands(0, v, total)
        face.add(k - 1, 0, total)
        loads[k].wait()
        for c in CHUNKS:
            x_wait(k, c)
            outer(c, halo[k], v, *rest(k))
            x_start(k + 1, c)
        face.send(k, 0, v_at[k + 2])
        face.bands(1, v, total)
        face.add(k - 1, 1, total)
        inner(v, *rest(k))
    last = STEPS - 2
    face.send(last, 1, now3)
    face.bands(0, now3, total)
    face.bands(1, now3, total)
    face.add(last, 0, total)
    face.add(last, 1, total)
    loads[STEPS - 1].wait()
    for c in CHUNKS:
        x_wait(STEPS - 1, c)
    for k in range(1, STEPS):
        for c in CHUNKS:
            pl.when(at.right)(lambda: x_face(k, c, 0).wait_send())
            pl.when(at.left)(lambda: x_face(k, c, 1).wait_send())
    face.wait_sent(STEPS - 1)


def last_kernel(now2, now3, total, img_in, halo, cou, fwd, source,
                image_out, now_out, before_out, now4, img, sems):
    keep = pltpu.make_async_copy(now3, before_out, sems.at[0])
    keep.start()
    rest = (now2, now4, cou, fwd, img_in, img, (total, source.at[STEPS - 1]))
    copies = []

    def store(planes):
        for src, dst in ((now4, now_out), (img, image_out)):
            copies.append(pltpu.make_async_copy(src.at[planes], dst.at[planes], sems.at[1 + len(copies)]))
            copies[-1].start()

    for c in CHUNKS:
        outer(c, halo, now3, *rest)
    store(pl.ds(0, 4))
    store(pl.ds(CX - 4, 4))
    inner(now3, *rest)
    store(pl.ds(4, CX - 8))
    keep.wait()
    for copy in copies:
        copy.wait()


def local(courant, current, previous, image_in, forward_tt, traces, trace_owner, receiver_cell):
    dma = pltpu.SemaphoreType.DMA
    vmem, anywhere = pl.BlockSpec(memory_space=pltpu.VMEM), pl.BlockSpec(memory_space=pl.ANY)
    tile = pltpu.VMEM(TILE, F32)
    halo = pltpu.VMEM((2, 4, CY, CZ), F32)

    def kept(*arrays):
        return [pltpu.with_memory_space_constraint(a, pltpu.VMEM) for a in arrays]

    def far(*arrays):
        return [pltpu.with_memory_space_constraint(a, pltpu.HBM) for a in arrays]

    def edge_buffers(n):
        return [
            pltpu.VMEM((n, 2, 128, CZ), F32), pltpu.VMEM((n, 2, 128, CZ), F32),
            pltpu.VMEM((n, 2, CY, 128), F32), pltpu.VMEM((n, 2, CY, 128), F32),
        ]

    def edge_sems(n):
        return [dma((n, 4, 2)), dma((n, 4, 2)), dma((n, 2, 2)), dma((n, 2, 2)), dma((n, 2)), dma((n, 2))]

    outs = pl.pallas_call(
        first_kernel,
        out_shape=[
            tile, tile, tile, tile, tile, halo,
            pltpu.VMEM((CAP * STEPS, 128), F32), pltpu.VMEM((24, 128), I32),
            pltpu.VMEM((CZ, CZ), BF16), pltpu.VMEM((CY, 2 * CY), BF16), pltpu.VMEM((192, 192), BF16),
            pltpu.VMEM((64, 64), BF16), pltpu.VMEM((128, 128), BF16),
        ],
        in_specs=[anywhere] * 7,
        out_specs=[vmem] * 13,
        scratch_shapes=[
            pltpu.VMEM((STEPS, RECS), F32), pltpu.VMEM((1, RECS), I32), pltpu.VMEM((1, RECS), I32),
            pltpu.VMEM((16, 8, 128), F32), pltpu.VMEM((16, 8, 128), F32),
            pltpu.VMEM((8, 16, 128), F32), pltpu.VMEM((8, 16, 128), F32),
            *edge_buffers(1), dma((7,)), *edge_sems(1), dma((4,)),
        ],
        compiler_params=pltpu.CompilerParams(collective_id=0, has_side_effects=True, vmem_limit_bytes=8 * MIB),
    )(*far(current, previous, courant, image_in, traces.T, trace_owner.T, receiver_cell[None, :]))
    cur, prev, cou, img, total0, halo0, values, targets, *weights = outs

    source = pl.pallas_call(
        source_kernel,
        out_shape=pltpu.VMEM((STEPS,) + TILE, F32),
        in_specs=[vmem, anywhere],
        out_specs=vmem,
        scratch_shapes=[
            pltpu.VMEM((CX * 2 * CY, STEPS, 128), F32),
            pltpu.VMEM((128, CAP * STEPS, 128), F32),
            pltpu.SMEM((24, 128), I32),
            dma(()),
        ],
        compiler_params=pltpu.CompilerParams(vmem_limit_bytes=14 * MIB),
    )(*kept(values, targets))

    now2, now3, total, img, halo3, fwd3 = pl.pallas_call(
        step_kernel,
        out_shape=[tile, tile, tile, tile, halo, tile],
        in_specs=[vmem] * 4 + [anywhere] + [vmem] * 8,
        out_specs=[vmem] * 6,
        scratch_shapes=[
            pltpu.VMEM((STEPS - 1,) + TILE, F32), tile, pltpu.VMEM((2, 2, 4, CY, CZ), F32), *edge_buffers(STEPS - 1), dma((STEPS,)), *edge_sems(STEPS - 1),
        ],
        compiler_params=pltpu.CompilerParams(collective_id=1, has_side_effects=True, vmem_limit_bytes=16 * MIB),
    )(*kept(cur, prev, cou, img), *far(forward_tt), *kept(total0, halo0, source, *weights))

    whole = jax.ShapeDtypeStruct(TILE, F32)
    return pl.pallas_call(
        last_kernel,
        out_shape=(whole, whole, whole),
        in_specs=[vmem] * 8,
        out_specs=(anywhere,) * 3,
        scratch_shapes=[tile, tile, dma((8,))],
        compiler_params=pltpu.CompilerParams(vmem_limit_bytes=8 * MIB),
    )(*kept(now2, now3, total, img, halo3, cou, fwd3, source))


def solution(mesh):
    cells = P("gx", "gy", "gz")
    every = ("gx", "gy", "gz")
    return jax.shard_map(
        local,
        mesh=mesh,
        in_specs=(cells, cells, cells, cells, P(None, "gx", "gy", "gz"), P(every, None), P(every, None), P(every)),
        out_specs=(cells, cells, cells),
        check_vma=False,
    )
```

```python
from types import SimpleNamespace

import jax
import jax.numpy as jnp
from jax import lax
from jax.experimental import pallas as pl
from jax.experimental.pallas import tpu as pltpu
from jax.sharding import PartitionSpec as P

STEPS = 4
CAP = 8
CX, CY, CZ = 32, 64, 256
N_GX, N_GY, N_GZ = 16, 4, 2
RECS = 256
ROWS = 16
CHUNKS = (1, 2, 0, 3)
SCALE = 5040.0
TAPS = (0.0, 8064.0, -1008.0, 128.0, -9.0)
CENTRE = -43050.0
F32, BF16, I32 = jnp.float32, jnp.bfloat16, jnp.int32
MESH = pl.DeviceIdType.MESH


def split(v):
    hi = v.astype(BF16)
    return hi, (v - hi.astype(F32)).astype(BF16)


def tap_of(distance):
    out = jnp.zeros(distance.shape, F32)
    for offset in range(1, 5):
        out = jnp.where(distance == offset, TAPS[offset], out)
    return out


def dot(a, b):
    return lax.dot_general(a, b, (((1,), (0,)), ((), ())), preferred_element_type=F32)


def iota(shape, dim):
    return lax.broadcasted_iota(I32, shape, dim)


PARTS = ((0, 7), (1, 2, 3, 4, 5, 6))
PAIRS = ((0, 1, 14, 15), tuple(range(2, 14)))
Y_ROWS = ((0, 32), (32, 96))
Z_ROWS = ((48, 16), (0, 48))
TILE = (CX, CY, CZ)
MIB = 1024 * 1024


def pick_from(values, i):
    out = i + values[0]
    for n in range(1, len(values)):
        if values[n] != values[n - 1] + 1:
            out = jnp.where(i >= n, i - n + values[n], out)
    return out


def edges(n, shift, downward):
    r_, c_ = iota((n, n), 0), iota((n, n), 1)
    same = (c_ // 4) == lax.rem(r_ // 4 + shift, n // 4)
    gap = lax.rem(r_, 4) - lax.rem(c_, 4)
    gap = jnp.where(downward, gap, -gap)
    return jnp.where(same & (gap >= 0), tap_of(4 - gap), 0.0)


def place():
    at = SimpleNamespace(gx=lax.axis_index("gx"), gy=lax.axis_index("gy"), gz=lax.axis_index("gz"))
    at.right, at.left = at.gx < N_GX - 1, at.gx > 0
    at.up, at.down = at.gy < N_GY - 1, at.gy > 0
    return at


def faces(at, ys, yr, zs, zr, ys_sem, yr_sem, zs_sem, zr_sem, weights):
    band_z, band_y, edge_y, edge_y_few, edge_z = weights
    block_of_lane = iota((CY, 128), 1) // 4
    own_block = lax.rem(block_of_lane + 32 - at.gz, 32)
    inside = block_of_lane == 31 * (1 - at.gz)
    last_lanes = iota((16, 128), 1) >= 96
    row8 = iota((8, CZ), 0)
    half = pl.ds(pl.multiple_of((1 - at.gz) * 128, 128), 128)

    def y_copy(n, part, side):
        rows = pl.ds(*Y_ROWS[part])
        return pltpu.make_async_remote_copy(
            src_ref=ys.at[n, side, rows], dst_ref=yr.at[n, side, rows],
            send_sem=ys_sem.at[n, part, side], recv_sem=yr_sem.at[n, part, side],
            device_id=(at.gx, at.gy + 1 if side == 0 else at.gy - 1, at.gz), device_id_type=MESH)

    def z_copy(n, part):
        rows = pl.ds(*Z_ROWS[part])
        return pltpu.make_async_remote_copy(
            src_ref=zs.at[n, rows], dst_ref=zr.at[n, rows],
            send_sem=zs_sem.at[n, part], recv_sem=zr_sem.at[n, part],
            device_id=(at.gx, at.gy, 1 - at.gz), device_id_type=MESH)

    def clear(slots):
        @pl.when(at.gy == 0)
        def _():
            for n in range(slots):
                yr[n, 0] = jnp.zeros(yr.shape[2:], F32)

        @pl.when(at.gy == N_GY - 1)
        def _():
            for n in range(slots):
                yr[n, 1] = jnp.zeros(yr.shape[2:], F32)

    def send(n, part, v):
        edge = jnp.zeros((CY, 128), F32)
        for i, x in enumerate(4 * g + j for g in PARTS[part] for j in range(4)):
            moved = pltpu.roll(v[x, :, half], 4 * i + 4, 1)
            edge = jnp.where(own_block == i, moved, edge)
        hi, lo = split(edge)
        sums = dot(hi, edge_z[...]) + dot(lo, edge_z[...])
        if part == 0:
            few = sums[0:16]
            for q in range(1, 4):
                few = few + pltpu.roll(sums[16 * q:16 * q + 16], 32 * q, 1)
        else:
            few = []
            for q in range(3):
                rest = pltpu.roll(sums[48:64], 96 - 32 * q, 1)
                few.append(jnp.where(last_lanes, rest, sums[16 * q:16 * q + 16]))
            few = jnp.concatenate(few, axis=0)
        first, count = Z_ROWS[part]
        zs[n, first:first + count, :] = few
        z_copy(n, part).start()

        first, count = Y_ROWS[part]
        packed_rows = []
        for p in PAIRS[part]:
            a, b = v[2 * p, CY - 8:CY, :], v[2 * p + 1, CY - 8:CY, :]
            packed_rows.append(jnp.where(row8 < 4, pltpu.roll(a, 4, 0), b))
        for p in PAIRS[part]:
            a, b = v[2 * p, 0:8, :], v[2 * p + 1, 0:8, :]
            packed_rows.append(jnp.where(row8 < 4, a, pltpu.roll(b, 4, 0)))
        hi, lo = split(jnp.concatenate(packed_rows, axis=0))
        matrix = edge_y[...] if part else edge_y_few[...]
        sums = dot(matrix, hi) + dot(matrix, lo)
        for side in range(2):
            ys[n, side, first:first + count, :] = sums[side * count:(side + 1) * count]
        pl.when(at.up)(lambda: y_copy(n, part, 0).start())
        pl.when(at.down)(lambda: y_copy(n, part, 1).start())


    def add(n, part, total):
        pl.when(at.down)(lambda: y_copy(n, part, 0).wait_recv())
        pl.when(at.up)(lambda: y_copy(n, part, 1).wait_recv())
        z_copy(n, part).wait_recv()
        first, count = Y_ROWS[part]
        for i, p in enumerate(PAIRS[part]):
            top = yr[n, 0, first + i * 8:first + i * 8 + 8, :]
            end = yr[n, 1, first + i * 8:first + i * 8 + 8, :]
            total[2 * p, 0:8, :] += jnp.where(row8 < 4, top, 0.0)
            total[2 * p + 1, 0:8, :] += jnp.where(row8 < 4, pltpu.roll(top, 4, 0), 0.0)
            total[2 * p, CY - 8:CY, :] += jnp.where(row8 < 4, 0.0, pltpu.roll(end, 4, 0))
            total[2 * p + 1, CY - 8:CY, :] += jnp.where(row8 < 4, 0.0, end)
        first, count = Z_ROWS[part]
        got = zr[n, first:first + count, :]
        if part == 0:
            got = jnp.concatenate([got] + [pltpu.roll(got, 128 - 32 * q, 1) for q in range(1, 4)], axis=0)
        else:
            rest = pltpu.roll(got[0:16], 32, 1)
            for q in range(1, 3):
                rest = jnp.where(iota((16, 128), 1) // 32 == q, pltpu.roll(got[16 * q:16 * q + 16], 32 + 32 * q, 1), rest)
            got = jnp.concatenate([got, rest], axis=0)
        got = pltpu.roll(got, 124 * (1 - at.gz), 1)
        for i, x in enumerate(4 * g + j for g in PARTS[part] for j in range(4)):
            moved = pltpu.roll(got, (128 - 4 * i) % 128, 1)
            total[x, :, half] += jnp.where(inside, moved, 0.0)

    def wait_sent(slots):
        for n in range(slots):
            for part in range(2):
                pl.when(at.up)(lambda: y_copy(n, part, 0).wait_send())
                pl.when(at.down)(lambda: y_copy(n, part, 1).wait_send())
                z_copy(n, part).wait_send()

    def bands(part, v_at, total, first=0, end=None):
        def body(i, carry):
            g = pick_from(PARTS[part], i)
            v = v_at[pl.ds(4 * g, 4)].reshape(4 * CY, CZ)
            hi, lo = split(v)
            here = dot(hi, band_z[...]) + dot(lo, band_z[...]) + CENTRE * v
            for p in (0, 2):
                one, two = slice(p * CY, (p + 1) * CY), slice((p + 1) * CY, (p + 2) * CY)
                both = jnp.concatenate([hi[one], lo[one], hi[two], lo[two]], axis=0)
                sums = here[p * CY:(p + 2) * CY] + dot(band_y[...], both)
                total[pl.ds(4 * g + p, 2)] = sums.reshape(2, CY, CZ)
            return carry
        lax.fori_loop(first, end or len(PARTS[part]), body, 0, unroll=2)

    return SimpleNamespace(clear=clear, send=send, add=add, wait_sent=wait_sent, bands=bands)


def x_copy(at, src, dst, sems, k, c, side):
    rows = pl.ds(c * ROWS, ROWS)
    planes = pl.ds(CX - 4, 4) if side == 0 else pl.ds(0, 4)
    return pltpu.make_async_remote_copy(
        src_ref=src.at[planes, rows], dst_ref=dst.at[side, :, rows],
        send_sem=sems[0].at[k, c, side], recv_sem=sems[1].at[k, c, side],
        device_id=(at.gx + 1 if side == 0 else at.gx - 1, at.gy, at.gz), device_id_type=MESH)


def first_kernel(current, previous, courant, image_in, forward, traces, owners, cells,
                 cur, prev, cou, img, fwd0, total, halo, field_a, field_b, values, targets,
                 band_z, band_y, edge_y, edge_y_few, edge_z,
                 tr, ow, ce, packed, r1, t1, r2, ys, yr, zs, zr,
                 in_sem, xs_sem, xr_sem, ys_sem, yr_sem, zs_sem, zr_sem, route_sem):
    at = place()
    group = at.gy * N_GZ + at.gz
    loads = [
        pltpu.make_async_copy(traces, tr, in_sem.at[0]),
        pltpu.make_async_copy(owners, ow, in_sem.at[1]),
        pltpu.make_async_copy(cells, ce, in_sem.at[2]),
        pltpu.make_async_copy(current, cur, in_sem.at[3]),
        pltpu.make_async_copy(courant, cou, in_sem.at[4]),
        pltpu.make_async_copy(previous, prev, in_sem.at[5]),
        pltpu.make_async_copy(image_in, img, in_sem.at[6]),
        pltpu.make_async_copy(forward.at[0], fwd0, in_sem.at[7]),
    ]
    for load in loads[:4]:
        load.start()

    barrier = pltpu.get_barrier_semaphore()

    def in_group(offset):
        other = lax.rem(group + offset, N_GY * N_GZ)
        return other, (at.gx, other // N_GZ, lax.rem(other, N_GZ))

    def in_line(offset):
        other = lax.rem(at.gx + offset, N_GX)
        return other, (other, at.gy, at.gz)

    def greet_group(o, carry):
        pl.semaphore_signal(barrier, inc=1, device_id=in_group(o)[1], device_id_type=MESH)
        return carry

    def greet_line(o, carry):
        pl.semaphore_signal(barrier, inc=1, device_id=in_line(o)[1], device_id_type=MESH)
        return carry

    lax.fori_loop(1, 16, greet_line, 0)
    lax.fori_loop(1, 8, greet_group, 0)

    r_, c_ = iota((CZ, CZ), 0), iota((CZ, CZ), 1)
    band_z[...] = tap_of(jnp.abs(r_ - c_)).astype(BF16)
    r_, c_ = iota((2 * CY, 4 * CY), 0), iota((2 * CY, 4 * CY), 1)
    gap = jnp.abs(lax.rem(r_, CY) - lax.rem(c_, CY))
    band_y[...] = jnp.where(r_ // CY == c_ // (2 * CY), tap_of(gap), 0.0).astype(BF16)
    edge_z[...] = edges(128, 31 * at.gz, at.gz == 0).astype(BF16)
    for matrix, n in ((edge_y_few, 64), (edge_y, 192)):
        upward = iota((n, n), 0) < n // 2
        matrix[...] = edges(n, 0, ~upward).astype(BF16)

    for load in loads[:3]:
        load.wait()
    owner = ow[...]
    cell = ce[...]
    row = cell // CZ
    field = [None] * 16
    for k in range(STEPS):
        hi, lo = split(tr[k:k + 1, :] * SCALE)
        field[k], field[4 + k] = hi.astype(F32), lo.astype(F32)
    field[8] = (row // 256).astype(F32)
    field[9] = (row % 256).astype(F32)
    field[10] = (cell % CZ).astype(F32)
    field[11] = jnp.ones((1, RECS), F32)
    zero = jnp.zeros((1, RECS), F32)
    field = jnp.concatenate([zero if f is None else f for f in field], axis=0)
    fields = jnp.concatenate([field] * 8, axis=0)
    owner_f = owner.astype(F32)
    owner_col = jnp.transpose(jnp.broadcast_to(owner_f, (128, RECS)))[:, :1]
    earlier = (owner_col == owner_f) & (iota((RECS, RECS), 0) < iota((RECS, RECS), 1))
    rank = jnp.sum(jnp.where(earlier, 1.0, 0.0), axis=0, keepdims=True)
    mine = iota((128, RECS), 0) == owner
    lane_block = iota((128, RECS), 0) // 16
    sums = jnp.zeros((128, 128), F32)
    for j in range(CAP):
        pick = jnp.where(mine & (rank == float(j)), 1.0, 0.0).astype(BF16)
        part = jnp.where(lane_block == j, fields, 0.0).astype(BF16)
        sums = sums + lax.dot_general(pick, part, (((1,), (1,)), ((), ())), preferred_element_type=F32)
    packed[...] = sums.reshape(16, 8, 128)

    pl.semaphore_wait(barrier, 22)

    def send_line(o, carry):
        other, device = in_line(o)
        pltpu.make_async_remote_copy(
            src_ref=packed.at[other], dst_ref=r1.at[o], send_sem=route_sem.at[0], recv_sem=route_sem.at[1],
            device_id=device, device_id_type=MESH).start()
        return carry

    lax.fori_loop(1, 16, send_line, 0)

    def x_face(c, side):
        return x_copy(at, current, halo, (xs_sem, xr_sem), 0, c, side)

    for c in CHUNKS:
        pl.when(at.right)(lambda: x_face(c, 0).start())
        pl.when(at.left)(lambda: x_face(c, 1).start())
    r1[0] = packed[at.gx]

    face = faces(at, ys, yr, zs, zr, ys_sem, yr_sem, zs_sem, zr_sem,
                 (band_z, band_y, edge_y, edge_y_few, edge_z))
    face.clear(1)
    pl.when(~at.left)(lambda: halo.__setitem__(0, jnp.zeros(halo.shape[1:], F32)))
    pl.when(~at.right)(lambda: halo.__setitem__(1, jnp.zeros(halo.shape[1:], F32)))

    loads[3].wait()
    for load in loads[4:]:
        load.start()
    face.send(0, 0, cur)
    face.send(0, 1, cur)
    for field in (field_a, field_b):
        rows = field.reshape(CX * 2 * CY * STEPS, 128)

        def blank(i, carry):
            rows[pl.ds(pl.multiple_of(i * 512, 512), 512), :] = jnp.zeros((512, 128), F32)
            return carry
        lax.fori_loop(0, CX * 2 * CY * STEPS // 512, blank, 0)

    pltpu.make_async_copy(r1.at[pl.ds(1, 15)], r1.at[pl.ds(1, 15)], route_sem.at[1]).wait()
    for j in range(8):
        t1[j] = r1[:, j, :]

    def send_group(o, carry):
        other, device = in_group(o)
        pltpu.make_async_remote_copy(
            src_ref=t1.at[other], dst_ref=r2.at[o], send_sem=route_sem.at[2], recv_sem=route_sem.at[3],
            device_id=device, device_id_type=MESH).start()
        return carry

    lax.fori_loop(1, 8, send_group, 0)
    r2[0] = t1[group]

    face.bands(0, cur, total)
    face.bands(1, cur, total)
    loads[4].wait()

    def rescale(x, carry):
        cou[x] = cou[x] * (1.0 / SCALE)
        return carry
    lax.fori_loop(0, CX, rescale, 0)
    face.add(0, 0, total)
    face.add(0, 1, total)

    pltpu.make_async_copy(r2.at[pl.ds(1, 7)], r2.at[pl.ds(1, 7)], route_sem.at[3]).wait()
    got = jnp.transpose(r2[...].reshape(128, 128))
    for r in range(CAP):
        values[4 * r:4 * r + 4, :] = got[16 * r:16 * r + 4] + got[16 * r + 4:16 * r + 8]
        cell_row = (got[16 * r + 8:16 * r + 9] * 256.0 + got[16 * r + 9:16 * r + 10]).astype(I32)
        depth = got[16 * r + 10:16 * r + 11].astype(I32)
        targets[r:r + 1, :] = (cell_row // CY) * (2 * CY) + (depth // 128) * CY + cell_row % CY
        targets[CAP + r:CAP + r + 1, :] = depth % 128
    held = got[11:12]
    for r in range(1, CAP):
        held = held + got[16 * r + 11:16 * r + 12]
    targets[2 * CAP:2 * CAP + 1, :] = held.astype(I32)
    targets[2 * CAP + 1:, :] = jnp.zeros((7, 128), I32)

    for load in loads[5:]:
        load.wait()
    for c in CHUNKS:
        pl.when(at.left)(lambda: x_face(c, 0).wait_recv())
        pl.when(at.right)(lambda: x_face(c, 1).wait_recv())
        pl.when(at.right)(lambda: x_face(c, 0).wait_send())
        pl.when(at.left)(lambda: x_face(c, 1).wait_send())
    pltpu.make_async_copy(r1.at[pl.ds(1, 15)], r1.at[pl.ds(1, 15)], route_sem.at[0]).wait()
    pltpu.make_async_copy(r2.at[pl.ds(1, 7)], r2.at[pl.ds(1, 7)], route_sem.at[2]).wait()
    face.wait_sent(1)


def source_kernel(values, targets, blank_a, blank_b, field_a, field_b, spread, where, sem):
    del blank_a, blank_b
    fetch = pltpu.make_async_copy(targets, where, sem)
    fetch.start()
    for p in range(128):
        spread[p] = jnp.broadcast_to(values[:, p:p + 1], (CAP * STEPS, 128))
    fetch.wait()
    lanes = iota((STEPS, 128), 1)

    def put(p, r):
        for field, n in ((field_a, r), (field_b, r + 1)):
            row = where[n, p]
            part = jnp.where(lanes == where[CAP + n, p], spread[p, STEPS * n:STEPS * (n + 1), :], 0.0)
            field[row] = field[row] + part

    def one(p, carry):
        held = where[2 * CAP, p]
        put(p, 0)

        @pl.when(held > 2)
        def _():
            put(p, 2)

            @pl.when(held > 4)
            def _():
                put(p, 4)
                put(p, 6)
        return carry
    lax.fori_loop(0, 128, one, 0)


def source_at(fields, k, x, t):
    halves = []
    for h in range(2):
        rows = pl.ds(((x * 2 + h) * CY + t * 8) * STEPS + k, 8, stride=STEPS)
        halves.append(fields[0][rows, :] + fields[1][rows, :])
    return jnp.concatenate(halves, axis=1)


def update(k, planes, t, window, before, after, cou, fwd, image, image_after, total, fields):
    rows = pl.ds(pl.multiple_of(t * 8, 8), 8)
    for x in planes:
        v = window(x)
        here = total[x, rows, :]
        if fields:
            here = here + source_at(fields, k, x, t)
        for o in range(1, 5):
            here = here + TAPS[o] * (window(x - o) + window(x + o))
        new = (v + v) - before[x, rows, :] + cou[x, rows, :] * here
        after[x, rows, :] = new
        image_after[x, rows, :] = image[x, rows, :] + fwd[x, rows, :] * new


def inner(k, v, *rest):
    def body(t, carry):
        rows = pl.ds(pl.multiple_of(t * 8, 8), 8)
        planes = {x: v[x, rows, :] for x in range(CX)}
        update(k, range(4, CX - 4), t, lambda x: planes[x], *rest)
        return carry
    lax.fori_loop(0, CY // 8, body, 0)


def outer(k, c, halo, v, *rest):
    def body(t, carry):
        rows = pl.ds(pl.multiple_of(t * 8, 8), 8)
        for side in range(2):
            low = 0 if side == 0 else CX - 8
            planes = {x: v[x, rows, :] for x in range(low, low + 8)}
            for i in range(4):
                planes[i - 4 if side == 0 else CX + i] = halo[side, i, rows, :]
            here = range(0, 4) if side == 0 else range(CX - 4, CX)
            update(k, here, t, lambda x: planes[x], *rest)
        return carry
    lax.fori_loop(c * ROWS // 8, (c + 1) * ROWS // 8, body, 0)


def flat(*fields):
    return [field.reshape(CX * 2 * CY * STEPS, 128) for field in fields]


def step_kernel(cur, prev, cou, img_in, forward, fwd0, total0, halo0, field_a, field_b,
                band_z, band_y, edge_y, edge_y_few, edge_z,
                now2, now3, now4, total, img, halo3,
                fwd, now1, halos, ys, yr, zs, zr,
                in_sem, xs_sem, xr_sem, ys_sem, yr_sem, zs_sem, zr_sem):
    at = place()
    fwd_at = [fwd0, fwd.at[0], fwd.at[1], fwd.at[2]]
    loads = [pltpu.make_async_copy(forward.at[k], fwd_at[k], in_sem.at[k]) for k in range(1, STEPS)]
    for load in loads:
        load.start()
    barrier = pltpu.get_barrier_semaphore()

    def greet(x, y, z):
        pl.semaphore_signal(barrier, inc=1, device_id=(x, y, z), device_id_type=MESH)

    pl.when(at.right)(lambda: greet(at.gx + 1, at.gy, at.gz))
    pl.when(at.left)(lambda: greet(at.gx - 1, at.gy, at.gz))
    pl.when(at.up)(lambda: greet(at.gx, at.gy + 1, at.gz))
    pl.when(at.down)(lambda: greet(at.gx, at.gy - 1, at.gz))
    greet(at.gx, at.gy, 1 - at.gz)
    one = lambda yes: jnp.where(yes, 1, 0)
    neighbours = 1 + one(at.right) + one(at.left) + one(at.up) + one(at.down)

    v_at = [prev, cur, now1, now2, now3, now4]
    halo = [halo0, halos.at[0], halos.at[1], halo3]
    fields = flat(field_a, field_b)
    face = faces(at, ys, yr, zs, zr, ys_sem, yr_sem, zs_sem, zr_sem,
                 (band_z, band_y, edge_y, edge_y_few, edge_z))

    def rest(k):
        first = k == 0
        return (v_at[k], v_at[k + 2], cou, fwd_at[k], img_in if first else img, img, total0 if first else total, fields)

    def x_face(k, c, side):
        return x_copy(at, v_at[k + 1], halo[k], (xs_sem, xr_sem), k - 1, c, side)

    def x_start(k, c):
        pl.when(at.right)(lambda: x_face(k, c, 0).start())
        pl.when(at.left)(lambda: x_face(k, c, 1).start())

    def x_wait(k, c):
        pl.when(at.left)(lambda: x_face(k, c, 0).wait_recv())
        pl.when(at.right)(lambda: x_face(k, c, 1).wait_recv())

    face.clear(STEPS - 1)
    for k in range(1, STEPS):
        pl.when(~at.left)(lambda: halo[k].__setitem__(0, jnp.zeros(halo3.shape[1:], F32)))
        pl.when(~at.right)(lambda: halo[k].__setitem__(1, jnp.zeros(halo3.shape[1:], F32)))

    def last_sources():
        def body(t, carry):
            rows = pl.ds(pl.multiple_of(t * 8, 8), 8)
            for x in (0, 1, 2, 3, CX - 4, CX - 3, CX - 2, CX - 1):
                total[x, rows, :] += source_at(fields, STEPS - 1, x, t)
            return carry
        lax.fori_loop(0, CY // 8, body, 0)

    for c in CHUNKS:
        outer(0, c, halo0, cur, *rest(0))
    pl.semaphore_wait(barrier, neighbours)
    for c in CHUNKS:
        x_start(1, c)
    face.send(0, 0, now1)
    inner(0, cur, *rest(0))
    for k in range(1, STEPS):
        v = v_at[k + 1]
        face.send(k - 1, 1, v)
        face.bands(0, v, total)
        face.bands(1, v, total)
        face.add(k - 1, 0, total)
        loads[k - 1].wait()
        if k < STEPS - 1:
            for c in CHUNKS:
                x_wait(k, c)
                outer(k, c, halo[k], v, *rest(k))
                x_start(k + 1, c)
            face.send(k, 0, v_at[k + 2])
        else:
            last_sources()
        face.add(k - 1, 1, total)
        inner(k, v, *rest(k))
    for c in CHUNKS:
        x_wait(STEPS - 1, c)
    for k in range(1, STEPS):
        for c in CHUNKS:
            pl.when(at.right)(lambda: x_face(k, c, 0).wait_send())
            pl.when(at.left)(lambda: x_face(k, c, 1).wait_send())
    face.wait_sent(STEPS - 1)


def last_kernel(now2, now3, now4_in, total, img_in, halo, cou, forward,
                image_out, now_out, before_out, fwd, now4, img, sems, in_sem):
    copies = []
    sides = (pl.ds(0, 4), pl.ds(CX - 4, 4))
    loads = [pltpu.make_async_copy(forward.at[STEPS - 1, planes], fwd.at[planes], in_sem.at[i]) for i, planes in enumerate(sides)]
    for load in loads:
        load.start()

    def store(src, dst, planes):
        copies.append(pltpu.make_async_copy(src.at[planes], dst.at[planes], sems.at[len(copies)]))
        copies[-1].start()

    store(now4_in, now_out, pl.ds(4, CX - 8))
    store(img_in, image_out, pl.ds(4, CX - 8))
    store(now3, before_out, pl.ds(0, CX))
    for load in loads:
        load.wait()
    for c in CHUNKS:
        outer(STEPS - 1, c, halo, now3, now2, now4, cou, fwd, img_in, img, total, None)
    for planes in sides:
        store(now4, now_out, planes)
        store(img, image_out, planes)
    for copy in copies:
        copy.wait()


def local(courant, current, previous, image_in, forward_tt, traces, trace_owner, receiver_cell):
    dma = pltpu.SemaphoreType.DMA
    vmem, anywhere = pl.BlockSpec(memory_space=pltpu.VMEM), pl.BlockSpec(memory_space=pl.ANY)
    tile = pltpu.VMEM(TILE, F32)
    halo = pltpu.VMEM((2, 4, CY, CZ), F32)
    field = pltpu.VMEM((CX * 2 * CY, STEPS, 128), F32)

    def kept(*arrays):
        return [pltpu.with_memory_space_constraint(a, pltpu.VMEM) for a in arrays]

    def far(*arrays):
        return [pltpu.with_memory_space_constraint(a, pltpu.HBM) for a in arrays]

    def edge_buffers(n):
        return [
            pltpu.VMEM((n, 2, 128, CZ), F32), pltpu.VMEM((n, 2, 128, CZ), F32),
            pltpu.VMEM((n, CY, 128), F32), pltpu.VMEM((n, CY, 128), F32),
        ]

    def edge_sems(n):
        return [dma((n, 4, 2)), dma((n, 4, 2)), dma((n, 2, 2)), dma((n, 2, 2)), dma((n, 2)), dma((n, 2))]

    outs = pl.pallas_call(
        first_kernel,
        out_shape=[
            tile, tile, tile, tile, tile, tile, halo,
            field, field,
            pltpu.VMEM((CAP * STEPS, 128), F32), pltpu.VMEM((24, 128), I32),
            pltpu.VMEM((CZ, CZ), BF16), pltpu.VMEM((2 * CY, 4 * CY), BF16), pltpu.VMEM((192, 192), BF16),
            pltpu.VMEM((64, 64), BF16), pltpu.VMEM((128, 128), BF16),
        ],
        in_specs=[anywhere] * 8,
        out_specs=[vmem] * 16,
        scratch_shapes=[
            pltpu.VMEM((STEPS, RECS), F32), pltpu.VMEM((1, RECS), I32), pltpu.VMEM((1, RECS), I32),
            pltpu.VMEM((16, 8, 128), F32), pltpu.VMEM((16, 8, 128), F32),
            pltpu.VMEM((8, 16, 128), F32), pltpu.VMEM((8, 16, 128), F32),
            *edge_buffers(1), dma((8,)), *edge_sems(1), dma((4,)),
        ],
        compiler_params=pltpu.CompilerParams(collective_id=0, has_side_effects=True, vmem_limit_bytes=8 * MIB),
    )(*far(current, previous, courant, image_in, forward_tt, traces.T, trace_owner.T, receiver_cell[None, :]))
    cur, prev, cou, img, fwd0, total0, halo0, field_a, field_b, values, targets, *weights = outs

    fields = pl.pallas_call(
        source_kernel,
        out_shape=[field, field],
        in_specs=[vmem, anywhere, vmem, vmem],
        out_specs=[vmem, vmem],
        input_output_aliases={2: 0, 3: 1},
        scratch_shapes=[
            pltpu.VMEM((128, CAP * STEPS, 128), F32),
            pltpu.SMEM((24, 128), I32),
            dma(()),
        ],
        compiler_params=pltpu.CompilerParams(vmem_limit_bytes=4 * MIB),
    )(*kept(values, targets, field_a, field_b))

    now2, now3, now4, total, img, halo3 = pl.pallas_call(
        step_kernel,
        out_shape=[tile, tile, tile, tile, tile, halo],
        in_specs=[vmem] * 4 + [anywhere] + [vmem] * 10,
        out_specs=[vmem] * 6,
        scratch_shapes=[
            pltpu.VMEM((STEPS - 1,) + TILE, F32), tile, pltpu.VMEM((2, 2, 4, CY, CZ), F32),
            *edge_buffers(STEPS - 1), dma((STEPS,)), *edge_sems(STEPS - 1),
        ],
        compiler_params=pltpu.CompilerParams(collective_id=1, has_side_effects=True, vmem_limit_bytes=13 * MIB),
    )(*kept(cur, prev, cou, img), *far(forward_tt), *kept(fwd0, total0, halo0, *fields, *weights))

    whole = jax.ShapeDtypeStruct(TILE, F32)
    return pl.pallas_call(
        last_kernel,
        out_shape=(whole, whole, whole),
        in_specs=[vmem] * 7 + [anywhere],
        out_specs=(anywhere,) * 3,
        scratch_shapes=[tile, tile, tile, dma((8,)), dma((2,))],
        compiler_params=pltpu.CompilerParams(vmem_limit_bytes=8 * MIB),
    )(*kept(now2, now3, now4, total, img, halo3, cou), *far(forward_tt))


def solution(mesh):
    cells = P("gx", "gy", "gz")
    every = ("gx", "gy", "gz")
    return jax.shard_map(
        local,
        mesh=mesh,
        in_specs=(cells, cells, cells, cells, P(None, "gx", "gy", "gz"), P(every, None), P(every, None), P(every)),
        out_specs=(cells, cells, cells),
        check_vma=False,
    )
```

```python
from types import SimpleNamespace

import jax
import jax.numpy as jnp
from jax import lax
from jax.experimental import pallas as pl
from jax.experimental.pallas import tpu as pltpu
from jax.sharding import PartitionSpec as P

STEPS = 4
CAP = 8
CX, CY, CZ = 32, 64, 256
N_GX, N_GY, N_GZ = 16, 4, 2
RECS = 256
ROWS = 16
CHUNKS = (0, 3, 1, 2)
SCALE = 5040.0
TAPS = (0.0, 8064.0, -1008.0, 128.0, -9.0)
CENTRE = -43050.0
F32, BF16, I32 = jnp.float32, jnp.bfloat16, jnp.int32
MESH = pl.DeviceIdType.MESH


def split(v):
    hi = v.astype(BF16)
    return hi, (v - hi.astype(F32)).astype(BF16)


def tap_of(distance):
    out = jnp.zeros(distance.shape, F32)
    for offset in range(1, 5):
        out = jnp.where(distance == offset, TAPS[offset], out)
    return out


def dot(a, b):
    return lax.dot_general(a, b, (((1,), (0,)), ((), ())), preferred_element_type=F32)


def iota(shape, dim):
    return lax.broadcasted_iota(I32, shape, dim)


PARTS = ((0, 7), (1, 2, 3, 4, 5, 6))
PAIRS = ((0, 1, 14, 15), tuple(range(2, 14)))
Y_ROWS = ((0, 32), (32, 96))
Z_ROWS = ((48, 32), (0, 48), (80, 32))
SPANS = {0: ((0, 16), (48, 16)), 2: ((16, 32),)}
TILE = (CX, CY, CZ)
MIB = 1024 * 1024


def pick_from(values, i):
    out = i + values[0]
    for n in range(1, len(values)):
        if values[n] != values[n - 1] + 1:
            out = jnp.where(i >= n, i - n + values[n], out)
    return out


def edges(n, shift, downward):
    r_, c_ = iota((n, n), 0), iota((n, n), 1)
    same = (c_ // 4) == lax.rem(r_ // 4 + shift, n // 4)
    gap = lax.rem(r_, 4) - lax.rem(c_, 4)
    gap = jnp.where(downward, gap, -gap)
    return jnp.where(same & (gap >= 0), tap_of(4 - gap), 0.0)


def place():
    at = SimpleNamespace(gx=lax.axis_index("gx"), gy=lax.axis_index("gy"), gz=lax.axis_index("gz"))
    at.right, at.left = at.gx < N_GX - 1, at.gx > 0
    at.up, at.down = at.gy < N_GY - 1, at.gy > 0
    return at


def faces(at, ys, yr, zs, zr, ys_sem, yr_sem, zs_sem, zr_sem, weights):
    band_z, band_y, edge_y, edge_y_few, edge_z = weights
    block_of_lane = iota((CY, 128), 1) // 4
    own_block = lax.rem(block_of_lane + 32 - at.gz, 32)
    inside = block_of_lane == 31 * (1 - at.gz)
    last_lanes = iota((16, 128), 1) >= 96
    row8 = iota((8, CZ), 0)
    half = pl.ds(pl.multiple_of((1 - at.gz) * 128, 128), 128)

    def y_copy(n, part, side):
        rows = pl.ds(*Y_ROWS[part])
        return pltpu.make_async_remote_copy(
            src_ref=ys.at[n, side, rows], dst_ref=yr.at[n, side, rows],
            send_sem=ys_sem.at[n, part, side], recv_sem=yr_sem.at[n, part, side],
            device_id=(at.gx, at.gy + 1 if side == 0 else at.gy - 1, at.gz), device_id_type=MESH)

    def z_copy(n, part):
        rows = pl.ds(*Z_ROWS[part])
        return pltpu.make_async_remote_copy(
            src_ref=zs.at[n, rows], dst_ref=zr.at[n, rows],
            send_sem=zs_sem.at[n, part], recv_sem=zr_sem.at[n, part],
            device_id=(at.gx, at.gy, 1 - at.gz), device_id_type=MESH)

    def clear(slots):
        @pl.when(at.gy == 0)
        def _():
            for n in range(slots):
                yr[n, 0] = jnp.zeros(yr.shape[2:], F32)

        @pl.when(at.gy == N_GY - 1)
        def _():
            for n in range(slots):
                yr[n, 1] = jnp.zeros(yr.shape[2:], F32)

    def send(n, part, v):
        if part == 1:
            edge = jnp.zeros((CY, 128), F32)
            for i, x in enumerate(range(4, CX - 4)):
                edge = jnp.where(own_block == i, pltpu.roll(v[x, :, half], 4 * i + 4, 1), edge)
        else:
            edge = jnp.zeros((32, 128), F32)
            for i, x in enumerate((0, 1, 2, 3, CX - 4, CX - 3, CX - 2, CX - 1)):
                rows = jnp.concatenate([v[x, at_row:at_row + rows, half] for at_row, rows in SPANS[part]], axis=0)
                edge = jnp.where(own_block[0:32] == i, pltpu.roll(rows, 4 * i + 4, 1), edge)
        hi, lo = split(edge)
        few = dot(hi, edge_z[...]) + dot(lo, edge_z[...])
        if part == 1:
            moved = [pltpu.roll(few[48:64], 96 - 32 * q, 1) for q in range(3)]
            few = jnp.concatenate([jnp.where(last_lanes, moved[q], few[16 * q:16 * q + 16]) for q in range(3)], axis=0)
        first, count = Z_ROWS[part]
        zs[n, first:first + count, :] = few
        z_copy(n, part).start()
        if part == 2:
            return

        first, count = Y_ROWS[part]
        packed_rows = []
        for p in PAIRS[part]:
            a, b = v[2 * p, CY - 8:CY, :], v[2 * p + 1, CY - 8:CY, :]
            packed_rows.append(jnp.where(row8 < 4, pltpu.roll(a, 4, 0), b))
        for p in PAIRS[part]:
            a, b = v[2 * p, 0:8, :], v[2 * p + 1, 0:8, :]
            packed_rows.append(jnp.where(row8 < 4, a, pltpu.roll(b, 4, 0)))
        hi, lo = split(jnp.concatenate(packed_rows, axis=0))
        matrix = edge_y[...] if part else edge_y_few[...]
        sums = dot(matrix, hi) + dot(matrix, lo)
        for side in range(2):
            ys[n, side, first:first + count, :] = sums[side * count:(side + 1) * count]
        pl.when(at.up)(lambda: y_copy(n, part, 0).start())
        pl.when(at.down)(lambda: y_copy(n, part, 1).start())


    def add(n, part, total):
        z_copy(n, part).wait_recv()
        first, count = Z_ROWS[part]
        got = zr[n, first:first + count, :]
        if part == 1:
            rest = pltpu.roll(got[0:16], 32, 1)
            for q in range(1, 3):
                rest = jnp.where(iota((16, 128), 1) // 32 == q, pltpu.roll(got[16 * q:16 * q + 16], 32 + 32 * q, 1), rest)
            got = jnp.concatenate([got, rest], axis=0)
        got = pltpu.roll(got, 124 * (1 - at.gz), 1)
        for i, x in enumerate(4 * g + j for g in PARTS[part % 2] for j in range(4)):
            moved = pltpu.roll(got, (128 - 4 * i) % 128, 1)
            moved = jnp.where(inside[0:moved.shape[0]], moved, 0.0)
            done = 0
            for at_row, rows in SPANS.get(part, ((0, CY),)):
                total[x, at_row:at_row + rows, half] += moved[done:done + rows]
                done += rows
        if part == 2:
            return

        pl.when(at.down)(lambda: y_copy(n, part, 0).wait_recv())
        pl.when(at.up)(lambda: y_copy(n, part, 1).wait_recv())
        first, count = Y_ROWS[part]
        for i, p in enumerate(PAIRS[part]):
            top = yr[n, 0, first + i * 8:first + i * 8 + 8, :]
            end = yr[n, 1, first + i * 8:first + i * 8 + 8, :]
            total[2 * p, 0:8, :] += jnp.where(row8 < 4, top, 0.0)
            total[2 * p + 1, 0:8, :] += jnp.where(row8 < 4, pltpu.roll(top, 4, 0), 0.0)
            total[2 * p, CY - 8:CY, :] += jnp.where(row8 < 4, 0.0, pltpu.roll(end, 4, 0))
            total[2 * p + 1, CY - 8:CY, :] += jnp.where(row8 < 4, 0.0, end)

    def wait_sent(slots):
        for n in range(slots):
            for part in range(2):
                pl.when(at.up)(lambda: y_copy(n, part, 0).wait_send())
                pl.when(at.down)(lambda: y_copy(n, part, 1).wait_send())
            for part in range(3):
                z_copy(n, part).wait_send()

    def bands(part, v_at, total, first=0, end=None):
        def body(i, carry):
            g = pick_from(PARTS[part], i)
            v = v_at[pl.ds(4 * g, 4)].reshape(4 * CY, CZ)
            hi, lo = split(v)
            here = dot(hi, band_z[...]) + dot(lo, band_z[...]) + CENTRE * v
            for p in (0, 2):
                one, two = slice(p * CY, (p + 1) * CY), slice((p + 1) * CY, (p + 2) * CY)
                both = jnp.concatenate([hi[one], lo[one], hi[two], lo[two]], axis=0)
                sums = here[p * CY:(p + 2) * CY] + dot(band_y[...], both)
                total[pl.ds(4 * g + p, 2)] = sums.reshape(2, CY, CZ)
            return carry
        lax.fori_loop(first, end or len(PARTS[part]), body, 0, unroll=2)

    return SimpleNamespace(clear=clear, send=send, add=add, wait_sent=wait_sent, bands=bands)


def x_copy(at, src, dst, sems, k, c, side):
    rows = pl.ds(c * ROWS, ROWS)
    planes = pl.ds(CX - 4, 4) if side == 0 else pl.ds(0, 4)
    return pltpu.make_async_remote_copy(
        src_ref=src.at[planes, rows], dst_ref=dst.at[side, :, rows],
        send_sem=sems[0].at[k, c, side], recv_sem=sems[1].at[k, c, side],
        device_id=(at.gx + 1 if side == 0 else at.gx - 1, at.gy, at.gz), device_id_type=MESH)


def first_kernel(current, previous, courant, image_in, forward, traces, owners, cells,
                 cur, prev, cou, img, fwd0, total, halo, field_a, field_b, values, targets,
                 band_z, band_y, edge_y, edge_y_few, edge_z,
                 tr, ow, ce, packed, r1, t1, r2, ys, yr, zs, zr,
                 in_sem, xs_sem, xr_sem, ys_sem, yr_sem, zs_sem, zr_sem, route_sem):
    at = place()
    group = at.gy * N_GZ + at.gz
    loads = [
        pltpu.make_async_copy(traces, tr, in_sem.at[0]),
        pltpu.make_async_copy(owners, ow, in_sem.at[1]),
        pltpu.make_async_copy(cells, ce, in_sem.at[2]),
        pltpu.make_async_copy(current, cur, in_sem.at[3]),
        pltpu.make_async_copy(courant, cou, in_sem.at[4]),
        pltpu.make_async_copy(previous, prev, in_sem.at[5]),
        pltpu.make_async_copy(image_in, img, in_sem.at[6]),
        pltpu.make_async_copy(forward.at[0], fwd0, in_sem.at[7]),
    ]
    for load in loads[:4]:
        load.start()

    barrier = pltpu.get_barrier_semaphore()

    def in_group(offset):
        other = lax.rem(group + offset, N_GY * N_GZ)
        return other, (at.gx, other // N_GZ, lax.rem(other, N_GZ))

    def in_line(offset):
        other = lax.rem(at.gx + offset, N_GX)
        return other, (other, at.gy, at.gz)

    def greet_group(o, carry):
        pl.semaphore_signal(barrier, inc=1, device_id=in_group(o)[1], device_id_type=MESH)
        return carry

    def greet_line(o, carry):
        pl.semaphore_signal(barrier, inc=1, device_id=in_line(o)[1], device_id_type=MESH)
        return carry

    lax.fori_loop(1, 16, greet_line, 0)
    lax.fori_loop(1, 8, greet_group, 0)

    r_, c_ = iota((CZ, CZ), 0), iota((CZ, CZ), 1)
    band_z[...] = tap_of(jnp.abs(r_ - c_)).astype(BF16)
    r_, c_ = iota((2 * CY, 4 * CY), 0), iota((2 * CY, 4 * CY), 1)
    gap = jnp.abs(lax.rem(r_, CY) - lax.rem(c_, CY))
    band_y[...] = jnp.where(r_ // CY == c_ // (2 * CY), tap_of(gap), 0.0).astype(BF16)
    edge_z[...] = edges(128, 31 * at.gz, at.gz == 0).astype(BF16)
    for matrix, n in ((edge_y_few, 64), (edge_y, 192)):
        upward = iota((n, n), 0) < n // 2
        matrix[...] = edges(n, 0, ~upward).astype(BF16)

    for load in loads[:3]:
        load.wait()
    owner = ow[...]
    cell = ce[...]
    row = cell // CZ
    field = [None] * 16
    for k in range(STEPS):
        hi, lo = split(tr[k:k + 1, :] * SCALE)
        field[k], field[4 + k] = hi.astype(F32), lo.astype(F32)
    field[8] = (row // 256).astype(F32)
    field[9] = (row % 256).astype(F32)
    field[10] = (cell % CZ).astype(F32)
    field[11] = jnp.ones((1, RECS), F32)
    zero = jnp.zeros((1, RECS), F32)
    field = jnp.concatenate([zero if f is None else f for f in field], axis=0)
    fields = jnp.concatenate([field] * 8, axis=0)
    owner_f = owner.astype(F32)
    owner_col = jnp.transpose(jnp.broadcast_to(owner_f, (128, RECS)))[:, :1]
    earlier = (owner_col == owner_f) & (iota((RECS, RECS), 0) < iota((RECS, RECS), 1))
    rank = jnp.sum(jnp.where(earlier, 1.0, 0.0), axis=0, keepdims=True)
    mine = iota((128, RECS), 0) == owner
    lane_block = iota((128, RECS), 0) // 16
    sums = jnp.zeros((128, 128), F32)
    for j in range(CAP):
        pick = jnp.where(mine & (rank == float(j)), 1.0, 0.0).astype(BF16)
        part = jnp.where(lane_block == j, fields, 0.0).astype(BF16)
        sums = sums + lax.dot_general(pick, part, (((1,), (1,)), ((), ())), preferred_element_type=F32)
    packed[...] = sums.reshape(16, 8, 128)

    pl.semaphore_wait(barrier, 22)

    def send_line(o, carry):
        other, device = in_line(o)
        pltpu.make_async_remote_copy(
            src_ref=packed.at[other], dst_ref=r1.at[o], send_sem=route_sem.at[0], recv_sem=route_sem.at[1],
            device_id=device, device_id_type=MESH).start()
        return carry

    lax.fori_loop(1, 16, send_line, 0)

    def x_face(c, side):
        return x_copy(at, current, halo, (xs_sem, xr_sem), 0, c, side)

    for c in CHUNKS:
        pl.when(at.right)(lambda: x_face(c, 0).start())
        pl.when(at.left)(lambda: x_face(c, 1).start())
    r1[0] = packed[at.gx]

    face = faces(at, ys, yr, zs, zr, ys_sem, yr_sem, zs_sem, zr_sem,
                 (band_z, band_y, edge_y, edge_y_few, edge_z))
    face.clear(1)
    pl.when(~at.left)(lambda: halo.__setitem__(0, jnp.zeros(halo.shape[1:], F32)))
    pl.when(~at.right)(lambda: halo.__setitem__(1, jnp.zeros(halo.shape[1:], F32)))

    loads[3].wait()
    for load in loads[4:]:
        load.start()
    face.send(0, 0, cur)
    face.send(0, 2, cur)
    face.send(0, 1, cur)
    for field in (field_a, field_b):
        rows = field.reshape(CX * 2 * CY * STEPS, 128)

        def blank(i, carry):
            rows[pl.ds(pl.multiple_of(i * 512, 512), 512), :] = jnp.zeros((512, 128), F32)
            return carry
        lax.fori_loop(0, CX * 2 * CY * STEPS // 512, blank, 0)

    pltpu.make_async_copy(r1.at[pl.ds(1, 15)], r1.at[pl.ds(1, 15)], route_sem.at[1]).wait()
    for j in range(8):
        t1[j] = r1[:, j, :]

    def send_group(o, carry):
        other, device = in_group(o)
        pltpu.make_async_remote_copy(
            src_ref=t1.at[other], dst_ref=r2.at[o], send_sem=route_sem.at[2], recv_sem=route_sem.at[3],
            device_id=device, device_id_type=MESH).start()
        return carry

    lax.fori_loop(1, 8, send_group, 0)
    r2[0] = t1[group]

    face.bands(0, cur, total)
    face.bands(1, cur, total)
    loads[4].wait()

    def rescale(x, carry):
        cou[x] = cou[x] * (1.0 / SCALE)
        return carry
    lax.fori_loop(0, CX, rescale, 0)
    face.add(0, 0, total)
    face.add(0, 2, total)
    face.add(0, 1, total)

    pltpu.make_async_copy(r2.at[pl.ds(1, 7)], r2.at[pl.ds(1, 7)], route_sem.at[3]).wait()
    got = jnp.transpose(r2[...].reshape(128, 128))
    for r in range(CAP):
        values[4 * r:4 * r + 4, :] = got[16 * r:16 * r + 4] + got[16 * r + 4:16 * r + 8]
        cell_row = (got[16 * r + 8:16 * r + 9] * 256.0 + got[16 * r + 9:16 * r + 10]).astype(I32)
        depth = got[16 * r + 10:16 * r + 11].astype(I32)
        targets[r:r + 1, :] = (cell_row // CY) * (2 * CY) + (depth // 128) * CY + cell_row % CY
        targets[CAP + r:CAP + r + 1, :] = depth % 128
    held = got[11:12]
    for r in range(1, CAP):
        held = held + got[16 * r + 11:16 * r + 12]
    targets[2 * CAP:2 * CAP + 1, :] = held.astype(I32)
    targets[2 * CAP + 1:, :] = jnp.zeros((7, 128), I32)

    for load in loads[5:]:
        load.wait()
    for c in CHUNKS:
        pl.when(at.left)(lambda: x_face(c, 0).wait_recv())
        pl.when(at.right)(lambda: x_face(c, 1).wait_recv())
        pl.when(at.right)(lambda: x_face(c, 0).wait_send())
        pl.when(at.left)(lambda: x_face(c, 1).wait_send())
    pltpu.make_async_copy(r1.at[pl.ds(1, 15)], r1.at[pl.ds(1, 15)], route_sem.at[0]).wait()
    pltpu.make_async_copy(r2.at[pl.ds(1, 7)], r2.at[pl.ds(1, 7)], route_sem.at[2]).wait()
    face.wait_sent(1)


def source_kernel(values, targets, blank_a, blank_b, field_a, field_b, spread, where, sem):
    del blank_a, blank_b
    fetch = pltpu.make_async_copy(targets, where, sem)
    fetch.start()
    for p in range(128):
        spread[p] = jnp.broadcast_to(values[:, p:p + 1], (CAP * STEPS, 128))
    fetch.wait()
    lanes = iota((STEPS, 128), 1)

    def put(p, r):
        for field, n in ((field_a, r), (field_b, r + 1)):
            row = where[n, p]
            part = jnp.where(lanes == where[CAP + n, p], spread[p, STEPS * n:STEPS * (n + 1), :], 0.0)
            field[row] = field[row] + part

    def one(p, carry):
        held = where[2 * CAP, p]
        put(p, 0)

        @pl.when(held > 2)
        def _():
            put(p, 2)

            @pl.when(held > 4)
            def _():
                put(p, 4)
                put(p, 6)
        return carry
    lax.fori_loop(0, 128, one, 0)


def source_at(fields, k, x, t):
    halves = []
    for h in range(2):
        rows = pl.ds(((x * 2 + h) * CY + t * 8) * STEPS + k, 8, stride=STEPS)
        halves.append(fields[0][rows, :] + fields[1][rows, :])
    return jnp.concatenate(halves, axis=1)


def update(k, planes, t, window, before, after, cou, fwd, image, image_after, total, fields):
    rows = pl.ds(pl.multiple_of(t * 8, 8), 8)
    for x in planes:
        v = window(x)
        here = total[x, rows, :]
        if fields:
            here = here + source_at(fields, k, x, t)
        for o in range(1, 5):
            here = here + TAPS[o] * (window(x - o) + window(x + o))
        new = (v + v) - before[x, rows, :] + cou[x, rows, :] * here
        after[x, rows, :] = new
        image_after[x, rows, :] = image[x, rows, :] + fwd[x, rows, :] * new


def inner(k, v, *rest):
    def body(t, carry):
        rows = pl.ds(pl.multiple_of(t * 8, 8), 8)
        planes = {x: v[x, rows, :] for x in range(CX)}
        update(k, range(4, CX - 4), t, lambda x: planes[x], *rest)
        return carry
    lax.fori_loop(0, CY // 8, body, 0)


def outer(k, c, halo, v, *rest):
    def body(t, carry):
        rows = pl.ds(pl.multiple_of(t * 8, 8), 8)
        for side in range(2):
            low = 0 if side == 0 else CX - 8
            planes = {x: v[x, rows, :] for x in range(low, low + 8)}
            for i in range(4):
                planes[i - 4 if side == 0 else CX + i] = halo[side, i, rows, :]
            here = range(0, 4) if side == 0 else range(CX - 4, CX)
            update(k, here, t, lambda x: planes[x], *rest)
        return carry
    lax.fori_loop(c * ROWS // 8, (c + 1) * ROWS // 8, body, 0)


def flat(*fields):
    return [field.reshape(CX * 2 * CY * STEPS, 128) for field in fields]


def step_kernel(cur, prev, cou, img_in, forward, fwd0, total0, halo0, field_a, field_b,
                band_z, band_y, edge_y, edge_y_few, edge_z,
                now2, now3, now4, total, img, halo3,
                fwd, now1, halos, ys, yr, zs, zr,
                in_sem, xs_sem, xr_sem, ys_sem, yr_sem, zs_sem, zr_sem):
    at = place()
    fwd_at = [fwd0, fwd.at[0], fwd.at[1], fwd.at[2]]
    loads = [pltpu.make_async_copy(forward.at[k], fwd_at[k], in_sem.at[k]) for k in range(1, STEPS)]
    for load in loads:
        load.start()
    barrier = pltpu.get_barrier_semaphore()

    def greet(x, y, z):
        pl.semaphore_signal(barrier, inc=1, device_id=(x, y, z), device_id_type=MESH)

    pl.when(at.right)(lambda: greet(at.gx + 1, at.gy, at.gz))
    pl.when(at.left)(lambda: greet(at.gx - 1, at.gy, at.gz))
    pl.when(at.up)(lambda: greet(at.gx, at.gy + 1, at.gz))
    pl.when(at.down)(lambda: greet(at.gx, at.gy - 1, at.gz))
    greet(at.gx, at.gy, 1 - at.gz)
    one = lambda yes: jnp.where(yes, 1, 0)
    neighbours = 1 + one(at.right) + one(at.left) + one(at.up) + one(at.down)

    v_at = [prev, cur, now1, now2, now3, now4]
    halo = [halo0, halos.at[0], halos.at[1], halo3]
    fields = flat(field_a, field_b)
    face = faces(at, ys, yr, zs, zr, ys_sem, yr_sem, zs_sem, zr_sem,
                 (band_z, band_y, edge_y, edge_y_few, edge_z))

    def rest(k):
        first = k == 0
        return (v_at[k], v_at[k + 2], cou, fwd_at[k], img_in if first else img, img, total0 if first else total, fields)

    def x_face(k, c, side):
        return x_copy(at, v_at[k + 1], halo[k], (xs_sem, xr_sem), k - 1, c, side)

    def x_start(k, c):
        pl.when(at.right)(lambda: x_face(k, c, 0).start())
        pl.when(at.left)(lambda: x_face(k, c, 1).start())

    def x_wait(k, c):
        pl.when(at.left)(lambda: x_face(k, c, 0).wait_recv())
        pl.when(at.right)(lambda: x_face(k, c, 1).wait_recv())

    def last_sources():
        def body(t, carry):
            rows = pl.ds(pl.multiple_of(t * 8, 8), 8)
            for x in (0, 1, 2, 3, CX - 4, CX - 3, CX - 2, CX - 1):
                total[x, rows, :] += source_at(fields, STEPS - 1, x, t)
            return carry
        lax.fori_loop(0, CY // 8, body, 0)

    pl.semaphore_wait(barrier, neighbours)
    for c in CHUNKS:
        outer(0, c, halo0, cur, *rest(0))
        x_start(1, c)
    face.clear(STEPS - 1)
    for k in range(1, STEPS):
        pl.when(~at.left)(lambda: halo[k].__setitem__(0, jnp.zeros(halo3.shape[1:], F32)))
        pl.when(~at.right)(lambda: halo[k].__setitem__(1, jnp.zeros(halo3.shape[1:], F32)))

    face.send(0, 0, now1)
    face.send(0, 2, now1)
    inner(0, cur, *rest(0))
    for k in range(1, STEPS - 1):
        v, then = v_at[k + 1], v_at[k + 2]

        def chunk(c):
            x_wait(k, c)
            outer(k, c, halo[k], v, *rest(k))
            x_start(k + 1, c)

        face.send(k - 1, 1, v)
        face.bands(0, v, total)
        loads[k - 1].wait()
        face.add(k - 1, 0, total)
        chunk(CHUNKS[0])
        face.bands(1, v, total, 0, 4)
        chunk(CHUNKS[1])
        face.send(k, 0, then)
        face.bands(1, v, total, 4, 6)
        face.add(k - 1, 2, total)
        chunk(CHUNKS[2])
        face.add(k - 1, 1, total)
        inner(k, v, *rest(k))
        chunk(CHUNKS[3])
        face.send(k, 2, then)
    last = STEPS - 2
    face.send(last, 1, now3)
    face.bands(0, now3, total)
    face.bands(1, now3, total)
    loads[last].wait()
    for part in (0, 2, 1):
        face.add(last, part, total)
    last_sources()
    inner(STEPS - 1, now3, *rest(STEPS - 1))
    for c in CHUNKS:
        x_wait(STEPS - 1, c)
    for k in range(1, STEPS):
        for c in CHUNKS:
            pl.when(at.right)(lambda: x_face(k, c, 0).wait_send())
            pl.when(at.left)(lambda: x_face(k, c, 1).wait_send())
    face.wait_sent(STEPS - 1)


def last_kernel(now2, now3, now4_in, total, img_in, halo, cou, forward,
                image_out, now_out, before_out, fwd, now4, img, sems, in_sem):
    copies = []
    sides = (pl.ds(0, 4), pl.ds(CX - 4, 4))
    loads = [pltpu.make_async_copy(forward.at[STEPS - 1, planes], fwd.at[planes], in_sem.at[i]) for i, planes in enumerate(sides)]
    for load in loads:
        load.start()

    def store(src, dst, planes):
        copies.append(pltpu.make_async_copy(src.at[planes], dst.at[planes], sems.at[len(copies)]))
        copies[-1].start()

    store(now4_in, now_out, pl.ds(4, CX - 8))
    store(img_in, image_out, pl.ds(4, CX - 8))
    store(now3, before_out, pl.ds(0, CX))
    for load in loads:
        load.wait()
    for c in CHUNKS:
        outer(STEPS - 1, c, halo, now3, now2, now4, cou, fwd, img_in, img, total, None)
    for planes in sides:
        store(now4, now_out, planes)
        store(img, image_out, planes)
    for copy in copies:
        copy.wait()


def local(courant, current, previous, image_in, forward_tt, traces, trace_owner, receiver_cell):
    dma = pltpu.SemaphoreType.DMA
    vmem, anywhere = pl.BlockSpec(memory_space=pltpu.VMEM), pl.BlockSpec(memory_space=pl.ANY)
    tile = pltpu.VMEM(TILE, F32)
    halo = pltpu.VMEM((2, 4, CY, CZ), F32)
    field = pltpu.VMEM((CX * 2 * CY, STEPS, 128), F32)

    def kept(*arrays):
        return [pltpu.with_memory_space_constraint(a, pltpu.VMEM) for a in arrays]

    def far(*arrays):
        return [pltpu.with_memory_space_constraint(a, pltpu.HBM) for a in arrays]

    def edge_buffers(n):
        return [
            pltpu.VMEM((n, 2, 128, CZ), F32), pltpu.VMEM((n, 2, 128, CZ), F32),
            pltpu.VMEM((n, 112, 128), F32), pltpu.VMEM((n, 112, 128), F32),
        ]

    def edge_sems(n):
        return [dma((n, 4, 2)), dma((n, 4, 2)), dma((n, 2, 2)), dma((n, 2, 2)), dma((n, 3)), dma((n, 3))]

    outs = pl.pallas_call(
        first_kernel,
        out_shape=[
            tile, tile, tile, tile, tile, tile, halo,
            field, field,
            pltpu.VMEM((CAP * STEPS, 128), F32), pltpu.VMEM((24, 128), I32),
            pltpu.VMEM((CZ, CZ), BF16), pltpu.VMEM((2 * CY, 4 * CY), BF16), pltpu.VMEM((192, 192), BF16),
            pltpu.VMEM((64, 64), BF16), pltpu.VMEM((128, 128), BF16),
        ],
        in_specs=[anywhere] * 8,
        out_specs=[vmem] * 16,
        scratch_shapes=[
            pltpu.VMEM((STEPS, RECS), F32), pltpu.VMEM((1, RECS), I32), pltpu.VMEM((1, RECS), I32),
            pltpu.VMEM((16, 8, 128), F32), pltpu.VMEM((16, 8, 128), F32),
            pltpu.VMEM((8, 16, 128), F32), pltpu.VMEM((8, 16, 128), F32),
            *edge_buffers(1), dma((8,)), *edge_sems(1), dma((4,)),
        ],
        compiler_params=pltpu.CompilerParams(collective_id=0, has_side_effects=True, vmem_limit_bytes=8 * MIB),
    )(*far(current, previous, courant, image_in, forward_tt, traces.T, trace_owner.T, receiver_cell[None, :]))
    cur, prev, cou, img, fwd0, total0, halo0, field_a, field_b, values, targets, *weights = outs

    fields = pl.pallas_call(
        source_kernel,
        out_shape=[field, field],
        in_specs=[vmem, anywhere, vmem, vmem],
        out_specs=[vmem, vmem],
        input_output_aliases={2: 0, 3: 1},
        scratch_shapes=[
            pltpu.VMEM((128, CAP * STEPS, 128), F32),
            pltpu.SMEM((24, 128), I32),
            dma(()),
        ],
        compiler_params=pltpu.CompilerParams(vmem_limit_bytes=4 * MIB),
    )(*kept(values, targets, field_a, field_b))

    now2, now3, now4, total, img, halo3 = pl.pallas_call(
        step_kernel,
        out_shape=[tile, tile, tile, tile, tile, halo],
        in_specs=[vmem] * 4 + [anywhere] + [vmem] * 10,
        out_specs=[vmem] * 6,
        scratch_shapes=[
            pltpu.VMEM((STEPS - 1,) + TILE, F32), tile, pltpu.VMEM((2, 2, 4, CY, CZ), F32),
            *edge_buffers(STEPS - 1), dma((STEPS,)), *edge_sems(STEPS - 1),
        ],
        compiler_params=pltpu.CompilerParams(collective_id=1, has_side_effects=True, vmem_limit_bytes=13 * MIB),
    )(*kept(cur, prev, cou, img), *far(forward_tt), *kept(fwd0, total0, halo0, *fields, *weights))

    whole = jax.ShapeDtypeStruct(TILE, F32)
    return pl.pallas_call(
        last_kernel,
        out_shape=(whole, whole, whole),
        in_specs=[vmem] * 7 + [anywhere],
        out_specs=(anywhere,) * 3,
        scratch_shapes=[tile, tile, tile, dma((8,)), dma((2,))],
        compiler_params=pltpu.CompilerParams(vmem_limit_bytes=8 * MIB),
    )(*kept(now2, now3, now4, total, img, halo3, cou), *far(forward_tt))


def solution(mesh):
    cells = P("gx", "gy", "gz")
    every = ("gx", "gy", "gz")
    return jax.shard_map(
        local,
        mesh=mesh,
        in_specs=(cells, cells, cells, cells, P(None, "gx", "gy", "gz"), P(every, None), P(every, None), P(every)),
        out_specs=(cells, cells, cells),
        check_vma=False,
    )
```

```python
from types import SimpleNamespace

import jax
import jax.numpy as jnp
from jax import lax
from jax.experimental import pallas as pl
from jax.experimental.pallas import tpu as pltpu
from jax.sharding import PartitionSpec as P

STEPS = 4
CAP = 8
CX, CY, CZ = 32, 64, 256
N_GX, N_GY, N_GZ = 16, 4, 2
RECS = 256
ROWS = 16
CHUNKS = (0, 3, 1, 2)
SCALE = 5040.0
TAPS = (0.0, 8064.0, -1008.0, 128.0, -9.0)
CENTRE = -43050.0
F32, BF16, I32 = jnp.float32, jnp.bfloat16, jnp.int32
MESH = pl.DeviceIdType.MESH


def split(v):
    hi = v.astype(BF16)
    return hi, (v - hi.astype(F32)).astype(BF16)


def tap_of(distance):
    out = jnp.zeros(distance.shape, F32)
    for offset in range(1, 5):
        out = jnp.where(distance == offset, TAPS[offset], out)
    return out


def dot(a, b):
    return lax.dot_general(a, b, (((1,), (0,)), ((), ())), preferred_element_type=F32)


def iota(shape, dim):
    return lax.broadcasted_iota(I32, shape, dim)


PARTS = ((0, 7), (1, 2, 3, 4, 5, 6))
PAIRS = ((0, 1, 14, 15), tuple(range(2, 14)))
Y_ROWS = ((0, 32), (32, 96))
Z_ROWS = ((48, 32), (0, 48), (80, 32))
SPANS = {0: ((0, 16), (48, 16)), 2: ((16, 32),)}
TILE = (CX, CY, CZ)
MIB = 1024 * 1024


def pick_from(values, i):
    out = i + values[0]
    for n in range(1, len(values)):
        if values[n] != values[n - 1] + 1:
            out = jnp.where(i >= n, i - n + values[n], out)
    return out


def edges(n, shift, downward):
    r_, c_ = iota((n, n), 0), iota((n, n), 1)
    same = (c_ // 4) == lax.rem(r_ // 4 + shift, n // 4)
    gap = lax.rem(r_, 4) - lax.rem(c_, 4)
    gap = jnp.where(downward, gap, -gap)
    return jnp.where(same & (gap >= 0), tap_of(4 - gap), 0.0)


def place():
    at = SimpleNamespace(gx=lax.axis_index("gx"), gy=lax.axis_index("gy"), gz=lax.axis_index("gz"))
    at.right, at.left = at.gx < N_GX - 1, at.gx > 0
    at.up, at.down = at.gy < N_GY - 1, at.gy > 0
    return at


def faces(at, ys, yr, zs, zr, ys_sem, yr_sem, zs_sem, zr_sem, weights):
    band_z, band_y, edge_y, edge_y_few, edge_z = weights
    block_of_lane = iota((CY, 128), 1) // 4
    own_block = lax.rem(block_of_lane + 32 - at.gz, 32)
    inside = block_of_lane == 31 * (1 - at.gz)
    last_lanes = iota((16, 128), 1) >= 96
    row8 = iota((8, CZ), 0)
    half = pl.ds(pl.multiple_of((1 - at.gz) * 128, 128), 128)

    def y_copy(n, part, side):
        rows = pl.ds(*Y_ROWS[part])
        return pltpu.make_async_remote_copy(
            src_ref=ys.at[n, side, rows], dst_ref=yr.at[n, side, rows],
            send_sem=ys_sem.at[n, part, side], recv_sem=yr_sem.at[n, part, side],
            device_id=(at.gx, at.gy + 1 if side == 0 else at.gy - 1, at.gz), device_id_type=MESH)

    def z_copy(n, part):
        rows = pl.ds(*Z_ROWS[part])
        return pltpu.make_async_remote_copy(
            src_ref=zs.at[n, rows], dst_ref=zr.at[n, rows],
            send_sem=zs_sem.at[n, part], recv_sem=zr_sem.at[n, part],
            device_id=(at.gx, at.gy, 1 - at.gz), device_id_type=MESH)

    def clear(slots):
        @pl.when(at.gy == 0)
        def _():
            for n in range(slots):
                yr[n, 0] = jnp.zeros(yr.shape[2:], F32)

        @pl.when(at.gy == N_GY - 1)
        def _():
            for n in range(slots):
                yr[n, 1] = jnp.zeros(yr.shape[2:], F32)

    def send(n, part, v):
        if part == 1:
            edge = jnp.zeros((CY, 128), F32)
            for i, x in enumerate(range(4, CX - 4)):
                edge = jnp.where(own_block == i, pltpu.roll(v[x, :, half], 4 * i + 4, 1), edge)
        else:
            edge = jnp.zeros((32, 128), F32)
            for i, x in enumerate((0, 1, 2, 3, CX - 4, CX - 3, CX - 2, CX - 1)):
                rows = jnp.concatenate([v[x, at_row:at_row + rows, half] for at_row, rows in SPANS[part]], axis=0)
                edge = jnp.where(own_block[0:32] == i, pltpu.roll(rows, 4 * i + 4, 1), edge)
        hi, lo = split(edge)
        few = dot(hi, edge_z[...]) + dot(lo, edge_z[...])
        if part == 1:
            moved = [pltpu.roll(few[48:64], 96 - 32 * q, 1) for q in range(3)]
            few = jnp.concatenate([jnp.where(last_lanes, moved[q], few[16 * q:16 * q + 16]) for q in range(3)], axis=0)
        first, count = Z_ROWS[part]
        zs[n, first:first + count, :] = few
        z_copy(n, part).start()
        if part == 2:
            return

        first, count = Y_ROWS[part]
        packed_rows = []
        for p in PAIRS[part]:
            a, b = v[2 * p, CY - 8:CY, :], v[2 * p + 1, CY - 8:CY, :]
            packed_rows.append(jnp.where(row8 < 4, pltpu.roll(a, 4, 0), b))
        for p in PAIRS[part]:
            a, b = v[2 * p, 0:8, :], v[2 * p + 1, 0:8, :]
            packed_rows.append(jnp.where(row8 < 4, a, pltpu.roll(b, 4, 0)))
        hi, lo = split(jnp.concatenate(packed_rows, axis=0))
        matrix = edge_y[...] if part else edge_y_few[...]
        sums = dot(matrix, hi) + dot(matrix, lo)
        for side in range(2):
            ys[n, side, first:first + count, :] = sums[side * count:(side + 1) * count]
        pl.when(at.up)(lambda: y_copy(n, part, 0).start())
        pl.when(at.down)(lambda: y_copy(n, part, 1).start())


    def add(n, part, total):
        z_copy(n, part).wait_recv()
        first, count = Z_ROWS[part]
        got = zr[n, first:first + count, :]
        if part == 1:
            rest = pltpu.roll(got[0:16], 32, 1)
            for q in range(1, 3):
                rest = jnp.where(iota((16, 128), 1) // 32 == q, pltpu.roll(got[16 * q:16 * q + 16], 32 + 32 * q, 1), rest)
            got = jnp.concatenate([got, rest], axis=0)
        got = pltpu.roll(got, 124 * (1 - at.gz), 1)
        for i, x in enumerate(4 * g + j for g in PARTS[part % 2] for j in range(4)):
            moved = pltpu.roll(got, (128 - 4 * i) % 128, 1)
            moved = jnp.where(inside[0:moved.shape[0]], moved, 0.0)
            done = 0
            for at_row, rows in SPANS.get(part, ((0, CY),)):
                total[x, at_row:at_row + rows, half] += moved[done:done + rows]
                done += rows
        if part == 2:
            return

        pl.when(at.down)(lambda: y_copy(n, part, 0).wait_recv())
        pl.when(at.up)(lambda: y_copy(n, part, 1).wait_recv())
        first, count = Y_ROWS[part]
        for i, p in enumerate(PAIRS[part]):
            top = yr[n, 0, first + i * 8:first + i * 8 + 8, :]
            end = yr[n, 1, first + i * 8:first + i * 8 + 8, :]
            total[2 * p, 0:8, :] += jnp.where(row8 < 4, top, 0.0)
            total[2 * p + 1, 0:8, :] += jnp.where(row8 < 4, pltpu.roll(top, 4, 0), 0.0)
            total[2 * p, CY - 8:CY, :] += jnp.where(row8 < 4, 0.0, pltpu.roll(end, 4, 0))
            total[2 * p + 1, CY - 8:CY, :] += jnp.where(row8 < 4, 0.0, end)

    def wait_sent(slots):
        for n in range(slots):
            for part in range(2):
                pl.when(at.up)(lambda: y_copy(n, part, 0).wait_send())
                pl.when(at.down)(lambda: y_copy(n, part, 1).wait_send())
            for part in range(3):
                z_copy(n, part).wait_send()

    def bands(part, v_at, total, first=0, end=None):
        def body(i, carry):
            g = pick_from(PARTS[part], i)
            v = v_at[pl.ds(4 * g, 4)].reshape(4 * CY, CZ)
            hi, lo = split(v)
            here = dot(hi, band_z[...]) + dot(lo, band_z[...]) + CENTRE * v
            for p in (0, 2):
                one, two = slice(p * CY, (p + 1) * CY), slice((p + 1) * CY, (p + 2) * CY)
                both = jnp.concatenate([hi[one], lo[one], hi[two], lo[two]], axis=0)
                sums = here[p * CY:(p + 2) * CY] + dot(band_y[...], both)
                total[pl.ds(4 * g + p, 2)] = sums.reshape(2, CY, CZ)
            return carry
        lax.fori_loop(first, end or len(PARTS[part]), body, 0, unroll=2)

    return SimpleNamespace(clear=clear, send=send, add=add, wait_sent=wait_sent, bands=bands)


def x_copy(at, src, dst, sems, k, c, side):
    rows = pl.ds(c * ROWS, ROWS)
    planes = pl.ds(CX - 4, 4) if side == 0 else pl.ds(0, 4)
    return pltpu.make_async_remote_copy(
        src_ref=src.at[planes, rows], dst_ref=dst.at[side, :, rows],
        send_sem=sems[0].at[k, c, side], recv_sem=sems[1].at[k, c, side],
        device_id=(at.gx + 1 if side == 0 else at.gx - 1, at.gy, at.gz), device_id_type=MESH)


def first_kernel(current, previous, courant, image_in, forward, traces, owners, cells,
                 cur, prev, cou, img, fwd0, total, halo, field_a, field_b, values, targets,
                 band_z, band_y, edge_y, edge_y_few, edge_z,
                 tr, ow, ce, packed, r1, t1, r2, ys, yr, zs, zr,
                 in_sem, xs_sem, xr_sem, ys_sem, yr_sem, zs_sem, zr_sem, route_sem):
    at = place()
    group = at.gy * N_GZ + at.gz
    loads = [
        pltpu.make_async_copy(traces, tr, in_sem.at[0]),
        pltpu.make_async_copy(owners, ow, in_sem.at[1]),
        pltpu.make_async_copy(cells, ce, in_sem.at[2]),
        pltpu.make_async_copy(current, cur, in_sem.at[3]),
        pltpu.make_async_copy(courant, cou, in_sem.at[4]),
        pltpu.make_async_copy(previous, prev, in_sem.at[5]),
        pltpu.make_async_copy(image_in, img, in_sem.at[6]),
        pltpu.make_async_copy(forward.at[0], fwd0, in_sem.at[7]),
    ]
    for load in loads[:4]:
        load.start()

    barrier = pltpu.get_barrier_semaphore()

    def in_group(offset):
        other = lax.rem(group + offset, N_GY * N_GZ)
        return other, (at.gx, other // N_GZ, lax.rem(other, N_GZ))

    def in_line(offset):
        other = lax.rem(at.gx + offset, N_GX)
        return other, (other, at.gy, at.gz)

    def greet_group(o, carry):
        pl.semaphore_signal(barrier, inc=1, device_id=in_group(o)[1], device_id_type=MESH)
        return carry

    def greet_line(o, carry):
        pl.semaphore_signal(barrier, inc=1, device_id=in_line(o)[1], device_id_type=MESH)
        return carry

    lax.fori_loop(1, 16, greet_line, 0)
    lax.fori_loop(1, 8, greet_group, 0)

    r_, c_ = iota((CZ, CZ), 0), iota((CZ, CZ), 1)
    band_z[...] = tap_of(jnp.abs(r_ - c_)).astype(BF16)
    r_, c_ = iota((2 * CY, 4 * CY), 0), iota((2 * CY, 4 * CY), 1)
    gap = jnp.abs(lax.rem(r_, CY) - lax.rem(c_, CY))
    band_y[...] = jnp.where(r_ // CY == c_ // (2 * CY), tap_of(gap), 0.0).astype(BF16)
    edge_z[...] = edges(128, 31 * at.gz, at.gz == 0).astype(BF16)
    for matrix, n in ((edge_y_few, 64), (edge_y, 192)):
        upward = iota((n, n), 0) < n // 2
        matrix[...] = edges(n, 0, ~upward).astype(BF16)

    for load in loads[:3]:
        load.wait()
    owner = ow[...]
    cell = ce[...]
    row = cell // CZ
    field = [None] * 16
    for k in range(STEPS):
        hi, lo = split(tr[k:k + 1, :] * SCALE)
        field[k], field[4 + k] = hi.astype(F32), lo.astype(F32)
    field[8] = (row // 256).astype(F32)
    field[9] = (row % 256).astype(F32)
    field[10] = (cell % CZ).astype(F32)
    field[11] = jnp.ones((1, RECS), F32)
    zero = jnp.zeros((1, RECS), F32)
    field = jnp.concatenate([zero if f is None else f for f in field], axis=0)
    fields = jnp.concatenate([field] * 8, axis=0)
    owner_f = owner.astype(F32)
    owner_col = jnp.transpose(jnp.broadcast_to(owner_f, (128, RECS)))[:, :1]
    earlier = (owner_col == owner_f) & (iota((RECS, RECS), 0) < iota((RECS, RECS), 1))
    rank = jnp.sum(jnp.where(earlier, 1.0, 0.0), axis=0, keepdims=True)
    mine = iota((128, RECS), 0) == owner
    lane_block = iota((128, RECS), 0) // 16
    sums = jnp.zeros((128, 128), F32)
    for j in range(CAP):
        pick = jnp.where(mine & (rank == float(j)), 1.0, 0.0).astype(BF16)
        part = jnp.where(lane_block == j, fields, 0.0).astype(BF16)
        sums = sums + lax.dot_general(pick, part, (((1,), (1,)), ((), ())), preferred_element_type=F32)
    packed[...] = sums.reshape(16, 8, 128)

    pl.semaphore_wait(barrier, 22)

    def send_line(o, carry):
        other, device = in_line(o)
        pltpu.make_async_remote_copy(
            src_ref=packed.at[other], dst_ref=r1.at[o], send_sem=route_sem.at[0], recv_sem=route_sem.at[1],
            device_id=device, device_id_type=MESH).start()
        return carry

    lax.fori_loop(1, 16, send_line, 0)

    def x_face(c, side):
        return x_copy(at, current, halo, (xs_sem, xr_sem), 0, c, side)

    for c in CHUNKS:
        pl.when(at.right)(lambda: x_face(c, 0).start())
        pl.when(at.left)(lambda: x_face(c, 1).start())
    r1[0] = packed[at.gx]

    face = faces(at, ys, yr, zs, zr, ys_sem, yr_sem, zs_sem, zr_sem,
                 (band_z, band_y, edge_y, edge_y_few, edge_z))
    face.clear(1)
    pl.when(~at.left)(lambda: halo.__setitem__(0, jnp.zeros(halo.shape[1:], F32)))
    pl.when(~at.right)(lambda: halo.__setitem__(1, jnp.zeros(halo.shape[1:], F32)))

    loads[3].wait()
    for load in loads[4:]:
        load.start()
    face.send(0, 0, cur)
    face.send(0, 2, cur)
    face.send(0, 1, cur)
    for field in (field_a, field_b):
        rows = field.reshape(CX * 2 * CY * STEPS, 128)

        def blank(i, carry):
            rows[pl.ds(pl.multiple_of(i * 512, 512), 512), :] = jnp.zeros((512, 128), F32)
            return carry
        lax.fori_loop(0, CX * 2 * CY * STEPS // 512, blank, 0)

    pltpu.make_async_copy(r1.at[pl.ds(1, 15)], r1.at[pl.ds(1, 15)], route_sem.at[1]).wait()
    for j in range(8):
        t1[j] = r1[:, j, :]

    def send_group(o, carry):
        other, device = in_group(o)
        pltpu.make_async_remote_copy(
            src_ref=t1.at[other], dst_ref=r2.at[o], send_sem=route_sem.at[2], recv_sem=route_sem.at[3],
            device_id=device, device_id_type=MESH).start()
        return carry

    lax.fori_loop(1, 8, send_group, 0)
    r2[0] = t1[group]

    face.bands(0, cur, total)
    face.bands(1, cur, total)
    loads[4].wait()

    def rescale(x, carry):
        cou[x] = cou[x] * (1.0 / SCALE)
        return carry
    lax.fori_loop(0, CX, rescale, 0)
    face.add(0, 0, total)
    face.add(0, 2, total)
    face.add(0, 1, total)

    pltpu.make_async_copy(r2.at[pl.ds(1, 7)], r2.at[pl.ds(1, 7)], route_sem.at[3]).wait()
    got = jnp.transpose(r2[...].reshape(128, 128))
    for r in range(CAP):
        values[4 * r:4 * r + 4, :] = got[16 * r:16 * r + 4] + got[16 * r + 4:16 * r + 8]
        cell_row = (got[16 * r + 8:16 * r + 9] * 256.0 + got[16 * r + 9:16 * r + 10]).astype(I32)
        depth = got[16 * r + 10:16 * r + 11].astype(I32)
        targets[r:r + 1, :] = (cell_row // CY) * (2 * CY) + (depth // 128) * CY + cell_row % CY
        targets[CAP + r:CAP + r + 1, :] = depth % 128
    held = got[11:12]
    for r in range(1, CAP):
        held = held + got[16 * r + 11:16 * r + 12]
    targets[2 * CAP:2 * CAP + 1, :] = held.astype(I32)
    targets[2 * CAP + 1:, :] = jnp.zeros((7, 128), I32)

    for load in loads[5:]:
        load.wait()
    for c in CHUNKS:
        pl.when(at.left)(lambda: x_face(c, 0).wait_recv())
        pl.when(at.right)(lambda: x_face(c, 1).wait_recv())
        pl.when(at.right)(lambda: x_face(c, 0).wait_send())
        pl.when(at.left)(lambda: x_face(c, 1).wait_send())
    pltpu.make_async_copy(r1.at[pl.ds(1, 15)], r1.at[pl.ds(1, 15)], route_sem.at[0]).wait()
    pltpu.make_async_copy(r2.at[pl.ds(1, 7)], r2.at[pl.ds(1, 7)], route_sem.at[2]).wait()
    face.wait_sent(1)


def source_kernel(values, targets, blank_a, blank_b, field_a, field_b, spread, where, sem):
    del blank_a, blank_b
    fetch = pltpu.make_async_copy(targets, where, sem)
    fetch.start()
    for p in range(128):
        spread[p] = jnp.broadcast_to(values[:, p:p + 1], (CAP * STEPS, 128))
    fetch.wait()
    lanes = iota((STEPS, 128), 1)

    def put(p, r):
        for field, n in ((field_a, r), (field_b, r + 1)):
            row = where[n, p]
            part = jnp.where(lanes == where[CAP + n, p], spread[p, STEPS * n:STEPS * (n + 1), :], 0.0)
            field[row] = field[row] + part

    def two(i, carry):
        pair = (2 * i, 2 * i + 1)
        held = jnp.maximum(where[2 * CAP, pair[0]], where[2 * CAP, pair[1]])
        for p in pair:
            put(p, 0)

        @pl.when(held > 2)
        def _():
            for p in pair:
                put(p, 2)

            @pl.when(held > 4)
            def _():
                for p in pair:
                    put(p, 4)
                    put(p, 6)
        return carry
    lax.fori_loop(0, 64, two, 0)


def source_at(fields, k, x, t):
    halves = []
    for h in range(2):
        rows = pl.ds(((x * 2 + h) * CY + t * 8) * STEPS + k, 8, stride=STEPS)
        halves.append(fields[0][rows, :] + fields[1][rows, :])
    return jnp.concatenate(halves, axis=1)


def update(k, planes, t, window, before, after, cou, fwd, image, image_after, total, fields):
    rows = pl.ds(pl.multiple_of(t * 8, 8), 8)
    for x in planes:
        v = window(x)
        here = total[x, rows, :]
        if fields:
            here = here + source_at(fields, k, x, t)
        for o in range(1, 5):
            here = here + TAPS[o] * (window(x - o) + window(x + o))
        new = (v + v) - before[x, rows, :] + cou[x, rows, :] * here
        after[x, rows, :] = new
        image_after[x, rows, :] = image[x, rows, :] + fwd[x, rows, :] * new


def inner(k, v, *rest):
    def body(t, carry):
        rows = pl.ds(pl.multiple_of(t * 8, 8), 8)
        planes = {x: v[x, rows, :] for x in range(CX)}
        update(k, range(4, CX - 4), t, lambda x: planes[x], *rest)
        return carry
    lax.fori_loop(0, CY // 8, body, 0)


def outer(k, c, halo, v, *rest):
    def body(t, carry):
        rows = pl.ds(pl.multiple_of(t * 8, 8), 8)
        for side in range(2):
            low = 0 if side == 0 else CX - 8
            planes = {x: v[x, rows, :] for x in range(low, low + 8)}
            for i in range(4):
                planes[i - 4 if side == 0 else CX + i] = halo[side, i, rows, :]
            here = range(0, 4) if side == 0 else range(CX - 4, CX)
            update(k, here, t, lambda x: planes[x], *rest)
        return carry
    lax.fori_loop(c * ROWS // 8, (c + 1) * ROWS // 8, body, 0)


def flat(*fields):
    return [field.reshape(CX * 2 * CY * STEPS, 128) for field in fields]


def step_kernel(cur, prev, cou, img_in, forward, fwd0, total0, halo0, field_a, field_b,
                band_z, band_y, edge_y, edge_y_few, edge_z,
                now2, now3, now4, total, img, halo3,
                fwd, now1, halos, ys, yr, zs, zr,
                in_sem, xs_sem, xr_sem, ys_sem, yr_sem, zs_sem, zr_sem):
    at = place()
    fwd_at = [fwd0, fwd.at[0], fwd.at[1], fwd.at[2]]
    loads = [pltpu.make_async_copy(forward.at[k], fwd_at[k], in_sem.at[k]) for k in range(1, STEPS)]
    for load in loads:
        load.start()
    barrier = pltpu.get_barrier_semaphore()

    def greet(x, y, z):
        pl.semaphore_signal(barrier, inc=1, device_id=(x, y, z), device_id_type=MESH)

    pl.when(at.right)(lambda: greet(at.gx + 1, at.gy, at.gz))
    pl.when(at.left)(lambda: greet(at.gx - 1, at.gy, at.gz))
    pl.when(at.up)(lambda: greet(at.gx, at.gy + 1, at.gz))
    pl.when(at.down)(lambda: greet(at.gx, at.gy - 1, at.gz))
    greet(at.gx, at.gy, 1 - at.gz)
    one = lambda yes: jnp.where(yes, 1, 0)
    neighbours = 1 + one(at.right) + one(at.left) + one(at.up) + one(at.down)

    v_at = [prev, cur, now1, now2, now3, now4]
    halo = [halo0, halos.at[0], halos.at[1], halo3]
    fields = flat(field_a, field_b)
    face = faces(at, ys, yr, zs, zr, ys_sem, yr_sem, zs_sem, zr_sem,
                 (band_z, band_y, edge_y, edge_y_few, edge_z))

    def rest(k):
        first = k == 0
        return (v_at[k], v_at[k + 2], cou, fwd_at[k], img_in if first else img, img, total0 if first else total, fields)

    def x_face(k, c, side):
        return x_copy(at, v_at[k + 1], halo[k], (xs_sem, xr_sem), k - 1, c, side)

    def x_start(k, c):
        pl.when(at.right)(lambda: x_face(k, c, 0).start())
        pl.when(at.left)(lambda: x_face(k, c, 1).start())

    def x_wait(k, c):
        pl.when(at.left)(lambda: x_face(k, c, 0).wait_recv())
        pl.when(at.right)(lambda: x_face(k, c, 1).wait_recv())

    def last_sources():
        def body(t, carry):
            rows = pl.ds(pl.multiple_of(t * 8, 8), 8)
            for x in (0, 1, 2, 3, CX - 4, CX - 3, CX - 2, CX - 1):
                total[x, rows, :] += source_at(fields, STEPS - 1, x, t)
            return carry
        lax.fori_loop(0, CY // 8, body, 0)

    pl.semaphore_wait(barrier, neighbours)
    for c in CHUNKS:
        outer(0, c, halo0, cur, *rest(0))
        x_start(1, c)
    face.clear(STEPS - 1)
    for k in range(1, STEPS):
        pl.when(~at.left)(lambda: halo[k].__setitem__(0, jnp.zeros(halo3.shape[1:], F32)))
        pl.when(~at.right)(lambda: halo[k].__setitem__(1, jnp.zeros(halo3.shape[1:], F32)))

    face.send(0, 0, now1)
    face.send(0, 2, now1)
    inner(0, cur, *rest(0))
    for k in range(1, STEPS - 1):
        v, then = v_at[k + 1], v_at[k + 2]

        def chunk(c):
            x_wait(k, c)
            outer(k, c, halo[k], v, *rest(k))
            x_start(k + 1, c)

        face.send(k - 1, 1, v)
        face.bands(0, v, total)
        loads[k - 1].wait()
        face.add(k - 1, 0, total)
        chunk(CHUNKS[0])
        face.bands(1, v, total, 0, 4)
        chunk(CHUNKS[1])
        face.send(k, 0, then)
        face.bands(1, v, total, 4, 6)
        face.add(k - 1, 2, total)
        chunk(CHUNKS[2])
        face.add(k - 1, 1, total)
        inner(k, v, *rest(k))
        chunk(CHUNKS[3])
        face.send(k, 2, then)
    last = STEPS - 2
    face.send(last, 1, now3)
    face.bands(0, now3, total)
    face.bands(1, now3, total)
    loads[last].wait()
    for part in (0, 2, 1):
        face.add(last, part, total)
    last_sources()
    inner(STEPS - 1, now3, *rest(STEPS - 1))
    for c in CHUNKS:
        x_wait(STEPS - 1, c)
    for k in range(1, STEPS):
        for c in CHUNKS:
            pl.when(at.right)(lambda: x_face(k, c, 0).wait_send())
            pl.when(at.left)(lambda: x_face(k, c, 1).wait_send())
    face.wait_sent(STEPS - 1)


def last_kernel(now2, now3, now4_in, total, img_in, halo, cou, forward,
                image_out, now_out, before_out, fwd, now4, img, sems, in_sem):
    copies = []
    sides = (pl.ds(0, 4), pl.ds(CX - 4, 4))
    loads = [pltpu.make_async_copy(forward.at[STEPS - 1, planes], fwd.at[planes], in_sem.at[i]) for i, planes in enumerate(sides)]
    for load in loads:
        load.start()

    def store(src, dst, planes):
        copies.append(pltpu.make_async_copy(src.at[planes], dst.at[planes], sems.at[len(copies)]))
        copies[-1].start()

    store(now4_in, now_out, pl.ds(4, CX - 8))
    store(img_in, image_out, pl.ds(4, CX - 8))
    store(now3, before_out, pl.ds(0, CX))
    for load in loads:
        load.wait()
    for c in CHUNKS:
        outer(STEPS - 1, c, halo, now3, now2, now4, cou, fwd, img_in, img, total, None)
    for planes in sides:
        store(now4, now_out, planes)
        store(img, image_out, planes)
    for copy in copies:
        copy.wait()


def local(courant, current, previous, image_in, forward_tt, traces, trace_owner, receiver_cell):
    dma = pltpu.SemaphoreType.DMA
    vmem, anywhere = pl.BlockSpec(memory_space=pltpu.VMEM), pl.BlockSpec(memory_space=pl.ANY)
    tile = pltpu.VMEM(TILE, F32)
    halo = pltpu.VMEM((2, 4, CY, CZ), F32)
    field = pltpu.VMEM((CX * 2 * CY, STEPS, 128), F32)

    def kept(*arrays):
        return [pltpu.with_memory_space_constraint(a, pltpu.VMEM) for a in arrays]

    def far(*arrays):
        return [pltpu.with_memory_space_constraint(a, pltpu.HBM) for a in arrays]

    def edge_buffers(n):
        return [
            pltpu.VMEM((n, 2, 128, CZ), F32), pltpu.VMEM((n, 2, 128, CZ), F32),
            pltpu.VMEM((n, 112, 128), F32), pltpu.VMEM((n, 112, 128), F32),
        ]

    def edge_sems(n):
        return [dma((n, 4, 2)), dma((n, 4, 2)), dma((n, 2, 2)), dma((n, 2, 2)), dma((n, 3)), dma((n, 3))]

    outs = pl.pallas_call(
        first_kernel,
        out_shape=[
            tile, tile, tile, tile, tile, tile, halo,
            field, field,
            pltpu.VMEM((CAP * STEPS, 128), F32), pltpu.VMEM((24, 128), I32),
            pltpu.VMEM((CZ, CZ), BF16), pltpu.VMEM((2 * CY, 4 * CY), BF16), pltpu.VMEM((192, 192), BF16),
            pltpu.VMEM((64, 64), BF16), pltpu.VMEM((128, 128), BF16),
        ],
        in_specs=[anywhere] * 8,
        out_specs=[vmem] * 16,
        scratch_shapes=[
            pltpu.VMEM((STEPS, RECS), F32), pltpu.VMEM((1, RECS), I32), pltpu.VMEM((1, RECS), I32),
            pltpu.VMEM((16, 8, 128), F32), pltpu.VMEM((16, 8, 128), F32),
            pltpu.VMEM((8, 16, 128), F32), pltpu.VMEM((8, 16, 128), F32),
            *edge_buffers(1), dma((8,)), *edge_sems(1), dma((4,)),
        ],
        compiler_params=pltpu.CompilerParams(collective_id=0, has_side_effects=True, vmem_limit_bytes=8 * MIB),
    )(*far(current, previous, courant, image_in, forward_tt, traces.T, trace_owner.T, receiver_cell[None, :]))
    cur, prev, cou, img, fwd0, total0, halo0, field_a, field_b, values, targets, *weights = outs

    fields = pl.pallas_call(
        source_kernel,
        out_shape=[field, field],
        in_specs=[vmem, anywhere, vmem, vmem],
        out_specs=[vmem, vmem],
        input_output_aliases={2: 0, 3: 1},
        scratch_shapes=[
            pltpu.VMEM((128, CAP * STEPS, 128), F32),
            pltpu.SMEM((24, 128), I32),
            dma(()),
        ],
        compiler_params=pltpu.CompilerParams(vmem_limit_bytes=4 * MIB),
    )(*kept(values, targets, field_a, field_b))

    now2, now3, now4, total, img, halo3 = pl.pallas_call(
        step_kernel,
        out_shape=[tile, tile, tile, tile, tile, halo],
        in_specs=[vmem] * 4 + [anywhere] + [vmem] * 10,
        out_specs=[vmem] * 6,
        scratch_shapes=[
            pltpu.VMEM((STEPS - 1,) + TILE, F32), tile, pltpu.VMEM((2, 2, 4, CY, CZ), F32),
            *edge_buffers(STEPS - 1), dma((STEPS,)), *edge_sems(STEPS - 1),
        ],
        compiler_params=pltpu.CompilerParams(collective_id=1, has_side_effects=True, vmem_limit_bytes=13 * MIB),
    )(*kept(cur, prev, cou, img), *far(forward_tt), *kept(fwd0, total0, halo0, *fields, *weights))

    whole = jax.ShapeDtypeStruct(TILE, F32)
    return pl.pallas_call(
        last_kernel,
        out_shape=(whole, whole, whole),
        in_specs=[vmem] * 7 + [anywhere],
        out_specs=(anywhere,) * 3,
        scratch_shapes=[tile, tile, tile, dma((8,)), dma((2,))],
        compiler_params=pltpu.CompilerParams(vmem_limit_bytes=8 * MIB),
    )(*kept(now2, now3, now4, total, img, halo3, cou), *far(forward_tt))


def solution(mesh):
    cells = P("gx", "gy", "gz")
    every = ("gx", "gy", "gz")
    return jax.shard_map(
        local,
        mesh=mesh,
        in_specs=(cells, cells, cells, cells, P(None, "gx", "gy", "gz"), P(every, None), P(every, None), P(every)),
        out_specs=(cells, cells, cells),
        check_vma=False,
    )
```
